256 devices in a mesh: ctx: 32 (over z, y), head: 8 (over x, core).
Axes of the slice: x: 4, y: 4, z: 8, core: 2. Of those that a mesh axis runs over, the one named last changes fastest.
Arguments:
- queries: bfloat16 [16384, 8192], P('ctx', 'head'), may hold values from -6 to 6
- keys: bfloat16 [16384, 1024], P('ctx', 'head'), may hold values from -5 to 5
- values: bfloat16 [16384, 1024], P('ctx', 'head'), may hold values from -6 to 6
- kept: int32 [8, 32, 64], P('head', 'ctx'), may hold values from 0 to 511, all different within a row
Outputs:
- attended: bfloat16 [16384, 8192], P('ctx', 'head')
The draws below stay inside these ranges and needn't reach their ends.
Inputs may be any that keep to these rules, and one draw needn't show every extreme that they name: Each row kept[h, c] names 64 distinct positions of host c's block.
All inputs are finite; a program needn't handle non-finite values.
Results may differ from the reference program's by a relative error of at most 0.0059.
Values may be sent and summed in bfloat16 or wider, within the bound.
A program may use at most 64 MiB of HBM per device.

```python
import jax
import jax.numpy as jnp
from jax import lax

HEAD_DIM = 128
QUERY_PER_KV = 8
KEY_HEADS = 8
BLOCK_TOKENS = 512
KEPT_POSITIONS = 64
ANCHOR_TOKENS = 256
CONTEXT_BLOCKS = 32
PROMPT_TOKENS = 16384


def draw_queries(key, part):
    key = jax.random.fold_in(key, 11)
    array_shape = (PROMPT_TOKENS, KEY_HEADS * QUERY_PER_KV * HEAD_DIM)
    final_output = jnp.clip(2.0 * jax.random.normal(key, array_shape, jnp.float32), -6.0, 6.0)
    return final_output.astype(jnp.bfloat16)


def draw_keys(key, part):
    key = jax.random.fold_in(key, 12)
    array_shape = (PROMPT_TOKENS, KEY_HEADS * HEAD_DIM)
    final_output = jnp.clip(jax.random.normal(key, array_shape, jnp.float32), -5.0, 5.0)
    return final_output.astype(jnp.bfloat16)


def steps_of(key, dims, cuts, smallest, top_value):
    def one(dim, blocks):
        steps = jax.random.uniform(jax.random.fold_in(jax.random.fold_in(key, 6), dim), (blocks,), jnp.float32, smallest / len(cuts), top_value / len(cuts))
        return jnp.repeat(jnp.exp(steps), dims[dim] // blocks).reshape((-1,) + (1,) * (len(dims) - dim - 1))

    factor_of = one(*cuts[0])
    for cut in cuts[1:]:
        factor_of = factor_of * one(*cut)
    return factor_of


def different_ones(stream_key, rows, count, top, lift):
    order = jax.random.permutation(jax.random.fold_in(stream_key, 1), count)
    boost = order
    for power in range(3):
        boost = boost * boost // count
    boost = boost * lift // count
    lots = jax.random.randint(jax.random.fold_in(stream_key, 2), (rows, count), 0, 4096) + boost
    sure = jax.random.permutation(jax.random.fold_in(stream_key, 3), rows)[jnp.arange(count) % rows]
    lots = jnp.where(jnp.arange(rows)[:, None] == sure[None, :], 1 << 14, lots)
    merit = lots * count + jnp.arange(count)
    return lax.top_k(merit.astype(jnp.int32), top)[1].astype(jnp.int32)


def scatter_about(rng, shape, scale, bound, shards=(), held_as=jnp.bfloat16):
    entries = scale * jax.random.normal(rng, shape, jnp.float32)
    if shards:
        entries = entries * steps_of(rng, shape, shards, -0.22, 0.18)
    return jnp.clip(entries, -bound, bound).astype(held_as)


def setup_inputs(seed: int = 0) -> dict:
    streams_of = jax.random.split(jax.random.key(seed), 5)
    queries = draw_queries(jax.random.fold_in(streams_of[4], 71), 0)
    keys = draw_keys(jax.random.fold_in(streams_of[4], 71), 0)
    values = scatter_about(streams_of[2], (PROMPT_TOKENS, KEY_HEADS * HEAD_DIM), 1.0, 6.0, ((0, 32), (1, 8)))
    kept = different_ones(streams_of[3], KEY_HEADS * CONTEXT_BLOCKS, BLOCK_TOKENS, KEPT_POSITIONS, 0).reshape((KEY_HEADS, CONTEXT_BLOCKS, KEPT_POSITIONS))
    return dict(queries=queries, keys=keys, values=values, kept=kept)


NEG = -1.0e30


def reference(queries, keys, values, kept):
    scale = HEAD_DIM ** -0.5
    row_items = BLOCK_TOKENS * QUERY_PER_KV
    blocked_keys = keys.reshape(CONTEXT_BLOCKS, BLOCK_TOKENS, KEY_HEADS, HEAD_DIM).transpose(2, 0, 1, 3)
    blocked_values = values.reshape(CONTEXT_BLOCKS, BLOCK_TOKENS, KEY_HEADS, HEAD_DIM).transpose(2, 0, 1, 3)
    selected_rows = kept[..., None]
    compact_keys = jnp.take_along_axis(blocked_keys, selected_rows, axis=2).reshape(KEY_HEADS, CONTEXT_BLOCKS * KEPT_POSITIONS, HEAD_DIM)
    compact_values = jnp.take_along_axis(blocked_values, selected_rows, axis=2).reshape(KEY_HEADS, CONTEXT_BLOCKS * KEPT_POSITIONS, HEAD_DIM)
    anchor_key_rows = keys[:ANCHOR_TOKENS].reshape(ANCHOR_TOKENS, KEY_HEADS, HEAD_DIM).transpose(1, 0, 2)
    anchor_value_rows = values[:ANCHOR_TOKENS].reshape(ANCHOR_TOKENS, KEY_HEADS, HEAD_DIM).transpose(1, 0, 2)
    query_matrix = queries.reshape(CONTEXT_BLOCKS, BLOCK_TOKENS, KEY_HEADS, QUERY_PER_KV, HEAD_DIM).transpose(0, 2, 1, 3, 4).reshape(CONTEXT_BLOCKS, KEY_HEADS, row_items, HEAD_DIM)
    key_source = jnp.arange(CONTEXT_BLOCKS * KEPT_POSITIONS, dtype=jnp.int32) // KEPT_POSITIONS
    row_token = jnp.arange(row_items, dtype=jnp.int32) // QUERY_PER_KV
    key_token = jnp.arange(BLOCK_TOKENS, dtype=jnp.int32)

    def one_head(args):
        qrows, akeys, avals, pkeys, pvals, okeys, ovals, context_block = args
        all_keys = jnp.concatenate([akeys, pkeys, okeys], axis=0)
        all_vals = jnp.concatenate([avals, pvals, ovals], axis=0)
        scores = jnp.dot(qrows, all_keys.T, preferred_element_type=jnp.float32) * scale
        front = jnp.concatenate([jnp.broadcast_to(context_block > 0, (ANCHOR_TOKENS,)), key_source < context_block])
        mask = jnp.concatenate([jnp.broadcast_to(front[None, :], (row_items, ANCHOR_TOKENS + CONTEXT_BLOCKS * KEPT_POSITIONS)),
                                key_token[None, :] <= row_token[:, None]], axis=1)
        top = jnp.max(jnp.where(mask, scores, NEG), axis=1)
        weight = jnp.where(mask, jnp.exp(scores - top[:, None]), 0.0)
        total = jnp.sum(weight, axis=1)
        numer = jnp.dot(weight.astype(jnp.bfloat16), all_vals, preferred_element_type=jnp.float32)
        return (numer / total[:, None]).astype(jnp.bfloat16)

    def one_host(context_block):
        head_list = jnp.full((KEY_HEADS,), context_block, dtype=jnp.int32)
        return lax.map(one_head, (query_matrix[context_block], anchor_key_rows, anchor_value_rows, compact_keys, compact_values,
                                  blocked_keys[:, context_block], blocked_values[:, context_block], head_list))

    final_output = lax.map(one_host, jnp.arange(CONTEXT_BLOCKS, dtype=jnp.int32))
    return final_output.reshape(CONTEXT_BLOCKS, KEY_HEADS, BLOCK_TOKENS, QUERY_PER_KV, HEAD_DIM).transpose(0, 2, 1, 3, 4).reshape(PROMPT_TOKENS, KEY_HEADS * QUERY_PER_KV * HEAD_DIM)
```

```python
import functools

import jax
import jax.numpy as jnp
from jax import lax
from jax.experimental import pallas as pl
from jax.experimental.pallas import tpu as pltpu
from jax.sharding import PartitionSpec as P

HEAD_DIM = 128
QUERY_PER_KV = 8
ANCHOR_TOKENS = 256
TILE = 256
PIECE = 16
LOG2_SCALE = HEAD_DIM**-0.5 * 1.4426950408889634
NEG = -1e30
F32, BF16 = jnp.float32, jnp.bfloat16


def scores_of(q2, k):
    k2 = jnp.concatenate([k, k], axis=1)
    return lax.dot_general(q2, k2, (((1,), (1,)), ((), ())), preferred_element_type=F32)


def weighted(p, v, ones):
    v2 = jnp.concatenate([v, ones], axis=1)
    return jnp.dot(p.astype(BF16), v2, preferred_element_type=F32)


def kernel(hosts, heads, q_hbm, k_ref, v_ref, kept_ref, o_hbm,
           q_buf, q2_buf, kv, ones_buf, mine, anchor, acc, top, o_buf,
           q_sem, o_sem, send_sem, recv_sem, hand_sem, pass_sem, anchor_sem):
    me = lax.axis_index("ctx")
    blk = k_ref.shape[0]
    ret = mine.shape[0]
    half = hosts // 2
    base = hosts * ret
    pieces = ANCHOR_TOKENS // PIECE
    first_relay = hosts // 4
    is_relay = (me >= first_relay) & (me < first_relay + pieces)
    chunks = blk // TILE
    rows = heads * TILE

    load_q = pltpu.make_async_copy(q_hbm, q_buf, q_sem)
    load_q.start()
    barrier = pltpu.get_barrier_semaphore()

    def greet(i, _):
        pl.semaphore_signal(barrier, inc=1, device_id={"ctx": lax.rem(me + i, hosts)},
                            device_id_type=pl.DeviceIdType.MESH)
        return 0

    lax.fori_loop(1, hosts, greet, 0)

    spots = lax.broadcasted_iota(jnp.int32, (blk, ret), 0)
    onehot = (kept_ref[0] == spots).astype(BF16)
    pick = (((0,), (0,)), ((), ()))
    mine[:, :HEAD_DIM] = lax.dot_general(onehot, k_ref[...], pick, preferred_element_type=F32).astype(BF16)
    mine[:, HEAD_DIM:] = lax.dot_general(onehot, v_ref[...], pick, preferred_element_type=F32).astype(BF16)

    @pl.when(me == 0)
    def _():
        anchor[:, :HEAD_DIM] = k_ref[:ANCHOR_TOKENS, :]
        anchor[:, HEAD_DIM:] = v_ref[:ANCHOR_TOKENS, :]

    first_key = jnp.broadcast_to(k_ref[0:1, :], (ret, HEAD_DIM))

    def blank(start):
        kv[pl.ds(start, ret), :HEAD_DIM] = first_key
        kv[pl.ds(start, ret), HEAD_DIM:] = jnp.zeros((ret, HEAD_DIM), BF16)
        ones_buf[pl.ds(start, ret), :] = jnp.zeros((ret, HEAD_DIM), BF16)

    def blank_slot(j, _):
        blank(pl.multiple_of(j * ret, ret))
        return 0

    def one_slot(j, _):
        ones_buf[pl.ds(pl.multiple_of(j * ret, ret), ret), :] = jnp.ones((ret, HEAD_DIM), BF16)
        return 0

    lax.fori_loop(0, me, one_slot, 0)
    lax.fori_loop(me, hosts, blank_slot, 0)

    @pl.when(me == 0)
    def _():
        for j in range(ANCHOR_TOKENS // ret):
            blank(base + j * ret)

    @pl.when(me > 0)
    def _():
        ones_buf[base:, :] = jnp.ones((ANCHOR_TOKENS, HEAD_DIM), BF16)

    pl.semaphore_wait(barrier, hosts - 1)

    def block_to(dst):
        slot = kv.at[pl.ds(pl.multiple_of(me * ret, ret), ret)]
        return pltpu.make_async_remote_copy(
            src_ref=mine, dst_ref=slot, send_sem=send_sem.at[dst], recv_sem=recv_sem.at[me],
            device_id={"ctx": dst}, device_id_type=pl.DeviceIdType.MESH)

    def block_from(src):
        slot = kv.at[pl.ds(pl.multiple_of(src * ret, ret), ret)]
        return pltpu.make_async_remote_copy(
            src_ref=mine, dst_ref=slot, send_sem=send_sem.at[src], recv_sem=recv_sem.at[src],
            device_id={"ctx": src}, device_id_type=pl.DeviceIdType.MESH)

    def hand(p):
        return pltpu.make_async_remote_copy(
            src_ref=anchor.at[pl.ds(pl.multiple_of(p * PIECE, PIECE), PIECE)],
            dst_ref=kv.at[pl.ds(pl.multiple_of(base + p * PIECE, PIECE), PIECE)],
            send_sem=hand_sem.at[p], recv_sem=anchor_sem.at[p],
            device_id={"ctx": first_relay + p}, device_id_type=pl.DeviceIdType.MESH)

    def passed(p, dst):
        piece = kv.at[pl.ds(pl.multiple_of(base + p * PIECE, PIECE), PIECE)]
        return pltpu.make_async_remote_copy(
            src_ref=piece, dst_ref=piece, send_sem=pass_sem.at[dst], recv_sem=anchor_sem.at[p],
            device_id={"ctx": dst}, device_id_type=pl.DeviceIdType.MESH)

    @pl.when(me == 0)
    def _():
        def go(p, _):
            hand(p).start()
            return 0

        lax.fori_loop(0, pieces, go, 0)

    def send(i, _):
        block_to(hosts - 1 - i).start()
        return 0

    lax.fori_loop(0, hosts - 1 - me, send, 0)

    load_q.wait()
    lower = lax.broadcasted_iota(jnp.int32, (TILE, TILE), 0) >= lax.broadcasted_iota(jnp.int32, (TILE, TILE), 1)

    def chunk_rows(c):
        return pl.ds(pl.multiple_of(c * rows, rows), rows)

    def store(c, newtop, newacc):
        top[chunk_rows(c), :] = jnp.broadcast_to(newtop, (rows, HEAD_DIM))
        acc[chunk_rows(c), :] = newacc

    def own(c):
        parts = [q_buf[c * TILE:(c + 1) * TILE, h * HEAD_DIM:(h + 1) * HEAD_DIM] for h in range(heads)]
        x = jnp.concatenate(parts, axis=0).astype(F32) * LOG2_SCALE
        high = x.astype(BF16)
        low = (x - high.astype(F32)).astype(BF16)
        q2 = jnp.concatenate([high, low], axis=1)
        q2_buf[chunk_rows(c), :] = q2
        ones = jnp.ones((TILE, HEAD_DIM), BF16)
        state = None
        for t in range(c, -1, -1):
            s = scores_of(q2, k_ref[t * TILE:(t + 1) * TILE, :])
            if t == c:
                s = jnp.where(jnp.concatenate([lower] * heads, axis=0), s, NEG)
            state = update(state, s, v_ref[t * TILE:(t + 1) * TILE, :], ones)
        store(c, *state)

    def update(state, s, v, ones):
        newtop = jnp.max(s, axis=1, keepdims=True)
        if state is None:
            return newtop, weighted(jnp.exp2(s - newtop), v, ones)
        oldtop, oldacc = state
        newtop = jnp.maximum(oldtop, newtop)
        d = weighted(jnp.exp2(s - newtop), v, ones)
        return newtop, oldacc * jnp.exp2(oldtop - newtop) + d

    def passing(c, tiles):
        q2 = q2_buf[chunk_rows(c), :]
        state = top[chunk_rows(c), 0:1], acc[chunk_rows(c), :]
        for t in tiles:
            at = slice(t * TILE, (t + 1) * TILE)
            state = update(state, scores_of(q2, kv[at, :HEAD_DIM]), kv[at, HEAD_DIM:], ones_buf[at, :])
        return state

    def arrive(lo, hi):
        def one(i, _):
            block_from(hi - 1 - i).wait_recv()
            return 0

        lax.fori_loop(0, hi - lo, one, 0)

    own(0)

    @pl.when(is_relay)
    def _():
        p = me - first_relay
        hand(p).wait_recv()

        def go(i, _):
            dst = lax.rem(me + i, hosts)

            @pl.when(dst > 0)
            def _():
                passed(p, dst).start()

            return 0

        lax.fori_loop(1, hosts, go, 0)

    for c in range(1, chunks):
        own(c)

    tiles = hosts * ret // TILE

    @pl.when(me > half)
    def _():
        arrive(half, me)
        for c in range(chunks):
            store(c, *passing(c, range(tiles - 1, tiles // 2 - 1, -1)))

    arrive(0, jnp.minimum(me, half))

    @pl.when(me > 0)
    def _():
        def one(p, _):
            @pl.when(p + first_relay != me)
            def _():
                hand(p).wait_recv()

            return 0

        lax.fori_loop(0, pieces, one, 0)

    last = list(range(tiles // 2 - 1, -1, -1)) + [tiles + i for i in range(ANCHOR_TOKENS // TILE)]
    outs = []
    for c in range(chunks):
        _, total = passing(c, last)
        o = (total[:, :HEAD_DIM] / total[:, HEAD_DIM:]).astype(BF16)
        for h in range(heads):
            o_buf[c * TILE:(c + 1) * TILE, h * HEAD_DIM:(h + 1) * HEAD_DIM] = o[h * TILE:(h + 1) * TILE]
        at = pl.ds(c * TILE, TILE)
        out = pltpu.make_async_copy(o_buf.at[at], o_hbm.at[at], o_sem.at[c])
        out.start()
        outs.append(out)

    def sent(i, _):
        block_to(hosts - 1 - i).wait_send()
        return 0

    lax.fori_loop(0, hosts - 1 - me, sent, 0)

    @pl.when(me == 0)
    def _():
        def one(p, _):
            hand(p).wait_send()
            return 0

        lax.fori_loop(0, pieces, one, 0)

    @pl.when(is_relay)
    def _():
        def one(i, _):
            dst = lax.rem(me + i, hosts)

            @pl.when(dst > 0)
            def _():
                passed(me - first_relay, dst).wait_send()

            return 0

        lax.fori_loop(1, hosts, one, 0)

    for out in outs:
        out.wait()


def on_device(hosts, queries, keys, values, kept):
    blk, width = queries.shape
    heads = width // HEAD_DIM
    ret = kept.shape[2]
    slots = hosts * ret + ANCHOR_TOKENS
    pieces = ANCHOR_TOKENS // PIECE
    vmem = pl.BlockSpec(memory_space=pltpu.VMEM)
    return pl.pallas_call(
        functools.partial(kernel, hosts, heads),
        out_shape=jax.ShapeDtypeStruct((blk, width), BF16),
        in_specs=[pl.BlockSpec(memory_space=pl.ANY), vmem, vmem, vmem],
        out_specs=pl.BlockSpec(memory_space=pl.ANY),
        scratch_shapes=[
            pltpu.VMEM((blk, width), BF16),
            pltpu.VMEM((blk * heads, 2 * HEAD_DIM), BF16),
            pltpu.VMEM((slots, 2 * HEAD_DIM), BF16),
            pltpu.VMEM((slots, HEAD_DIM), BF16),
            pltpu.VMEM((ret, 2 * HEAD_DIM), BF16),
            pltpu.VMEM((ANCHOR_TOKENS, 2 * HEAD_DIM), BF16),
            pltpu.VMEM((blk * heads, 2 * HEAD_DIM), F32),
            pltpu.VMEM((blk * heads, HEAD_DIM), F32),
            pltpu.VMEM((blk, width), BF16),
            pltpu.SemaphoreType.DMA,
            pltpu.SemaphoreType.DMA((blk // TILE,)),
            pltpu.SemaphoreType.DMA((hosts,)),
            pltpu.SemaphoreType.DMA((hosts,)),
            pltpu.SemaphoreType.DMA((pieces,)),
            pltpu.SemaphoreType.DMA((hosts,)),
            pltpu.SemaphoreType.DMA((pieces,)),
        ],
        compiler_params=pltpu.CompilerParams(
            collective_id=0, has_side_effects=True, vmem_limit_bytes=48 * 2**20),
    )(queries, keys, values, kept[0])


def solution(mesh):
    placed = (P("ctx", "head"), P("ctx", "head"), P("ctx", "head"), P("head", "ctx", None))
    return jax.shard_map(
        functools.partial(on_device, mesh.shape["ctx"]), mesh=mesh, in_specs=placed,
        out_specs=P("ctx", "head"), check_vma=False)
```

```python
import functools

import jax
import jax.numpy as jnp
from jax import lax
from jax.experimental import pallas as pl
from jax.experimental.pallas import tpu as pltpu
from jax.sharding import PartitionSpec as P

HEAD_DIM = 128
ANCHOR_TOKENS = 256
TILE = 256
RING = 4
LOG2_SCALE = HEAD_DIM**-0.5 * 1.4426950408889634
NEG = -1e30
F32, BF16 = jnp.float32, jnp.bfloat16
MESH = pl.DeviceIdType.MESH


def loop(lo, hi, body):
    def step(i, carry):
        body(i)
        return carry

    lax.fori_loop(lo, hi, step, 0)


def scores_of(q2, k):
    k2 = jnp.concatenate([k, k], axis=1)
    return lax.dot_general(q2, k2, (((1,), (1,)), ((), ())), preferred_element_type=F32)


def fold(state, s, v, ones):
    top = jnp.broadcast_to(jnp.max(s, axis=1, keepdims=True), (s.shape[0], HEAD_DIM))
    if state is not None:
        top = jnp.maximum(state[0], top)
    p = jnp.exp2(s - jnp.concatenate([top, top], axis=1)).astype(BF16)
    new = jnp.dot(p, jnp.concatenate([v, ones], axis=1), preferred_element_type=F32)
    if state is not None:
        factor = jnp.exp2(state[0] - top)
        new = state[1] * jnp.concatenate([factor, factor], axis=1) + new
    return top, new


def kernel(rows, heads, q_hbm, k_hbm, v_hbm, kept_hbm, o_ref,
           q_buf, k_buf, v_buf, kept_buf, q2_buf, kv, anchor, row_ones, mine, acc, top,
           in_sem, ready, z_send, a_send, z_recv, y_send, y_recv, h_send, h_recv, r_send, r_recv, hand_send):
    me = lax.axis_index("ctx")
    z, y = me // RING, me % RING
    blk = k_buf.shape[0]
    ret = mine.shape[0]
    half = ret // 2
    mid = rows // 2
    count = blk * heads
    both = heads * TILE
    own_level = rows

    loads = [pltpu.make_async_copy(a, b, in_sem.at[i]) for i, (a, b) in enumerate(
        [(kept_hbm, kept_buf), (k_hbm, k_buf), (v_hbm, v_buf), (q_hbm, q_buf)])]
    for load in loads:
        load.start()

    def at(zz, yy):
        return {"ctx": zz * RING + yy}

    barrier = pltpu.get_barrier_semaphore()
    for d in range(1, RING):
        pl.semaphore_signal(barrier, inc=1, device_id=at(z, (y + d) % RING), device_id_type=MESH)
    loop(z + 1, rows, lambda t: pl.semaphore_signal(barrier, inc=1, device_id=at(t, y), device_id_type=MESH))

    def slot(level, column, first=0, n=None):
        start = pl.multiple_of((level * RING + column) * ret + first, half)
        return kv.at[pl.ds(start, ret if n is None else n)]

    def remote(src, dst, send, recv, to):
        return pltpu.make_async_remote_copy(src_ref=src, dst_ref=dst, send_sem=send, recv_sem=recv,
                                            device_id=to, device_id_type=MESH)

    for load in loads[:3]:
        load.wait()
    spots = lax.broadcasted_iota(jnp.int32, (blk, ret), 0)
    onehot = (kept_buf[...] == spots).astype(BF16)
    pick = (((0,), (0,)), ((), ()))
    mine[:, :HEAD_DIM] = lax.dot_general(onehot, k_buf[...], pick, preferred_element_type=F32).astype(BF16)
    mine[:, HEAD_DIM:] = lax.dot_general(onehot, v_buf[...], pick, preferred_element_type=F32).astype(BF16)

    first_key = jnp.broadcast_to(k_buf[0:1, :], (ret, HEAD_DIM))

    def blank(c):
        r = pl.ds(pl.multiple_of((own_level * RING + c) * ret, ret), ret)
        kv[r, :HEAD_DIM] = first_key
        kv[r, HEAD_DIM:] = jnp.zeros((ret, HEAD_DIM), BF16)
        row_ones[pl.ds(pl.multiple_of(c * ret, ret), ret), :] = jnp.zeros((ret, HEAD_DIM), BF16)

    def filled(c):
        row_ones[pl.ds(pl.multiple_of(c * ret, ret), ret), :] = jnp.ones((ret, HEAD_DIM), BF16)

    loop(0, y, filled)
    loop(y, RING, blank)

    quarter = ANCHOR_TOKENS // RING

    @pl.when(me == 0)
    def _():
        anchor[:, :HEAD_DIM] = k_buf[:ANCHOR_TOKENS, :]
        anchor[:, HEAD_DIM:] = v_buf[:ANCHOR_TOKENS, :]
        kv[:quarter, :] = anchor[:quarter, :]

    def own():
        loads[3].wait()
        ones = jnp.ones((TILE, HEAD_DIM), BF16)
        lower = lax.broadcasted_iota(jnp.int32, (TILE, TILE), 0) >= lax.broadcasted_iota(jnp.int32, (TILE, TILE), 1)
        lower = jnp.concatenate([lower] * heads, axis=0)
        for c in range(blk // TILE):
            r = slice(c * both, (c + 1) * both)
            for h in range(heads):
                x = q_buf[c * TILE:(c + 1) * TILE, h * HEAD_DIM:(h + 1) * HEAD_DIM].astype(F32) * LOG2_SCALE
                high = x.astype(BF16)
                low = (x - high.astype(F32)).astype(BF16)
                q2_buf[c * both + h * TILE:c * both + (h + 1) * TILE, :] = jnp.concatenate([high, low], axis=1)
            q2 = q2_buf[r, :]
            state = None
            for t in range(c, -1, -1):
                s = scores_of(q2, k_buf[t * TILE:(t + 1) * TILE, :])
                if t == c:
                    s = jnp.where(lower, s, NEG)
                state = fold(state, s, v_buf[t * TILE:(t + 1) * TILE, :], ones)
            top[r, :], acc[r, :] = state

    def level_keys(level):
        tile = kv[pl.ds(pl.multiple_of(level * TILE, TILE), TILE), :]
        return tile[:, :HEAD_DIM], tile[:, HEAD_DIM:]

    def compute(level, ones):
        k, v = level_keys(level)
        top[...], acc[...] = fold((top[...], acc[...]), scores_of(q2_buf[...], k), v, ones)

    early = y < RING // 2

    @pl.when(early)
    def _():
        own()

    pl.semaphore_wait(barrier, z + RING - 1)
    loop(0, z, lambda t: pl.semaphore_signal(ready.at[z], inc=1, device_id=at(t, y), device_id_type=MESH))

    def hand(a):
        return remote(anchor.at[pl.ds(a * quarter, quarter)], slot(0, a), hand_send.at[a], z_recv.at[0], at(0, a))

    def to_row(c):
        return remote(mine, slot(own_level, y), r_send.at[c], r_recv.at[y], at(z, c))

    def from_row(c):
        return remote(mine, slot(own_level, c), r_send.at[c], r_recv.at[c], at(z, c))

    @pl.when(me == 0)
    def _():
        for a in range(1, RING):
            hand(a).start()

    loop(y + 1, RING, lambda c: to_row(c).start())

    def down(t):
        return remote(mine, slot(z + 1, y), z_send.at[t], z_recv.at[z + 1], at(t, y))

    def down_anchor(t):
        return remote(slot(0, y), slot(0, y), a_send.at[t], z_recv.at[0], at(t, y))

    def from_above(level):
        return remote(mine, slot(level, y), z_send.at[0], z_recv.at[level], at(z, (y + 1) % RING))

    @pl.when((z == 0) & (y > 0))
    def _():
        from_above(0).wait_recv()

    def send_down(t):
        pl.semaphore_wait(ready.at[t], 1)
        down(t).start()

        @pl.when(z == 0)
        def _():
            down_anchor(t).start()

    loop(z + 1, mid, send_down)
    last = rows - 1
    loop(0, jnp.minimum(last - z, rows - mid), lambda i: send_down(last - i))

    @pl.when(jnp.logical_not(early))
    def _():
        own()

    right, left, far = (y + 1) % RING, (y + RING - 1) % RING, (y + 2) % RING

    def level_of(i):
        h = i // 2
        return h + (1 - i % 2) * (z - 2 * h)

    def to_right(l):
        return remote(slot(l, y), slot(l, y), y_send.at[0, l], y_recv.at[0, l], at(z, right))

    def to_left(l):
        return remote(slot(l, y), slot(l, y), y_send.at[1, l], y_recv.at[1, l], at(z, left))

    def from_left(l):
        return remote(slot(l, left), slot(l, left), y_send.at[0, l], y_recv.at[0, l], at(z, left))

    def from_right(l):
        return remote(slot(l, right), slot(l, right), y_send.at[1, l], y_recv.at[1, l], at(z, right))

    def on_right(l):
        part = slot(l, left, 0, half)
        return remote(part, part, h_send.at[0, l], h_recv.at[0, l], at(z, right))

    def on_left(l):
        part = slot(l, right, half, half)
        return remote(part, part, h_send.at[1, l], h_recv.at[1, l], at(z, left))

    def far_left(l):
        part = slot(l, far, 0, half)
        return remote(part, part, h_send.at[0, l], h_recv.at[0, l], at(z, left))

    def far_right(l):
        part = slot(l, far, half, half)
        return remote(part, part, h_send.at[1, l], h_recv.at[1, l], at(z, right))

    def first(i):
        l = level_of(i)

        @pl.when(z > 0)
        def _():
            from_above(l).wait_recv()

        to_right(l).start()
        to_left(l).start()

    def second(i):
        l = level_of(i)
        from_left(l).wait_recv()
        on_right(l).start()
        from_right(l).wait_recv()
        on_left(l).start()

    def third(i):
        l = level_of(i)
        far_left(l).wait_recv()
        far_right(l).wait_recv()

    first(0)

    @pl.when(z > 0)
    def _():
        first(1)

    @pl.when(y > 0)
    def _():
        loop(0, y, lambda c: from_row(c).wait_recv())
        compute(own_level, row_ones[...])

    second(0)

    def step(i):
        @pl.when(i + 2 <= z)
        def _():
            first(i + 2)

        @pl.when(i + 1 <= z)
        def _():
            second(i + 1)

        third(i)

        @pl.when(me > 0)
        def _():
            compute(level_of(i), jnp.ones((TILE, HEAD_DIM), BF16))

    loop(0, z + 1, step)

    for c in range(blk // TILE):
        for h in range(heads):
            r = slice(c * both + h * TILE, c * both + (h + 1) * TILE)
            o_ref[c * TILE:(c + 1) * TILE, h * HEAD_DIM:(h + 1) * HEAD_DIM] = (
                acc[r, :HEAD_DIM] / acc[r, HEAD_DIM:]).astype(BF16)

    def gone(i):
        l = level_of(i)
        for copy in (to_right(l), to_left(l), on_right(l), on_left(l)):
            copy.wait_send()

    loop(0, z + 1, gone)
    loop(y + 1, RING, lambda c: to_row(c).wait_send())
    loop(z + 1, rows, lambda t: down(t).wait_send())

    @pl.when(z == 0)
    def _():
        loop(1, rows, lambda t: down_anchor(t).wait_send())

    @pl.when(me == 0)
    def _():
        for a in range(1, RING):
            hand(a).wait_send()


def on_device(hosts, queries, keys, values, kept):
    blk, width = queries.shape
    heads = width // HEAD_DIM
    ret = kept.shape[2]
    rows = hosts // RING
    hbm = pl.BlockSpec(memory_space=pltpu.HBM)
    dma = pltpu.SemaphoreType.DMA
    return pl.pallas_call(
        functools.partial(kernel, rows, heads),
        out_shape=pltpu.VMEM((blk, width), BF16),
        in_specs=[hbm] * 4,
        out_specs=pl.BlockSpec(memory_space=pltpu.VMEM),
        scratch_shapes=[
            pltpu.VMEM((blk, width), BF16),
            pltpu.VMEM((blk, HEAD_DIM), BF16),
            pltpu.VMEM((blk, HEAD_DIM), BF16),
            pltpu.VMEM((1, ret), jnp.int32),
            pltpu.VMEM((blk * heads, 2 * HEAD_DIM), BF16),
            pltpu.VMEM(((rows + 1) * TILE, 2 * HEAD_DIM), BF16),
            pltpu.VMEM((ANCHOR_TOKENS, 2 * HEAD_DIM), BF16),
            pltpu.VMEM((TILE, HEAD_DIM), BF16),
            pltpu.VMEM((ret, 2 * HEAD_DIM), BF16),
            pltpu.VMEM((blk * heads, 2 * HEAD_DIM), F32),
            pltpu.VMEM((blk * heads, HEAD_DIM), F32),
            dma((4,)),
            pltpu.SemaphoreType.REGULAR((rows,)),
            dma((rows,)), dma((rows,)), dma((rows,)),
            dma((2, rows)), dma((2, rows)), dma((2, rows)), dma((2, rows)),
            dma((RING,)), dma((RING,)), dma((RING,)),
        ],
        compiler_params=pltpu.CompilerParams(
            collective_id=0, has_side_effects=True, vmem_limit_bytes=61 * 2**20),
    )(queries, keys, values, kept[0])


def solution(mesh):
    placed = (P("ctx", "head"), P("ctx", "head"), P("ctx", "head"), P("head", "ctx", None))
    return jax.shard_map(
        functools.partial(on_device, mesh.shape["ctx"]), mesh=mesh, in_specs=placed,
        out_specs=P("ctx", "head"), check_vma=False)
```

```python
import functools

import jax
import jax.numpy as jnp
from jax import lax
from jax.experimental import pallas as pl
from jax.experimental.pallas import tpu as pltpu
from jax.sharding import PartitionSpec as P

HEAD_DIM = 128
ANCHOR_TOKENS = 256
TILE = 256
AHEAD = 4
RING = 4
LOG2_SCALE = HEAD_DIM**-0.5 * 1.4426950408889634
NEG = -1e30
F32, BF16 = jnp.float32, jnp.bfloat16
MESH = pl.DeviceIdType.MESH


def loop(lo, hi, body):
    def step(i, carry):
        body(i)
        return carry

    lax.fori_loop(lo, hi, step, 0)


def scores_of(q2, k):
    k2 = jnp.concatenate([k, k], axis=1)
    return lax.dot_general(q2, k2, (((1,), (1,)), ((), ())), preferred_element_type=F32)


def fold(state, s, v, ones):
    top = jnp.broadcast_to(jnp.max(s, axis=1, keepdims=True), (s.shape[0], HEAD_DIM))
    if state is not None:
        top = jnp.maximum(state[0], top)
    p = jnp.exp2(s - jnp.concatenate([top, top], axis=1)).astype(BF16)
    new = jnp.dot(p, jnp.concatenate([v, ones], axis=1), preferred_element_type=F32)
    if state is not None:
        factor = jnp.exp2(state[0] - top)
        new = state[1] * jnp.concatenate([factor, factor], axis=1) + new
    return top, new


def kernel(rows, heads, q_hbm, k_hbm, v_hbm, kept_hbm, o_ref,
           q_buf, k_buf, v_buf, kept_buf, q2_buf, kv, anchor, ones, mine, acc, top,
           in_sem, z_send, z_recv, y_send, y_recv, r_send, r_recv, hand_send, a_recv, a_send, ay_send, ay_recv):
    me = lax.axis_index("ctx")
    z, y = me // RING, me % RING
    blk = k_buf.shape[0]
    ret = mine.shape[0]
    both = heads * TILE
    last = rows - 1

    loads = [pltpu.make_async_copy(a, b, in_sem.at[i]) for i, (a, b) in enumerate(
        [(kept_hbm, kept_buf), (k_hbm, k_buf), (v_hbm, v_buf), (q_hbm, q_buf)])]
    for load in loads:
        load.start()

    def at(zz, yy):
        return {"ctx": zz * RING + yy}

    barrier = pltpu.get_barrier_semaphore()
    loop(0, z, lambda t: pl.semaphore_signal(barrier, inc=1, device_id=at(t, y), device_id_type=MESH))
    for d in range(1, RING):
        pl.semaphore_signal(barrier, inc=1, device_id=at(z, (y + d) % RING), device_id_type=MESH)

    def slot(n):
        return kv.at[pl.ds(pl.multiple_of(n * ret, ret), ret)]

    def column_slot(i):
        return slot(RING + i)

    def cross_slot(i, d):
        return slot(RING + z + (RING - 1) * i + d - 1)

    def remote(src, dst, send, recv, to):
        return pltpu.make_async_remote_copy(src_ref=src, dst_ref=dst, send_sem=send, recv_sem=recv,
                                            device_id=to, device_id_type=MESH)

    for load in loads[:3]:
        load.wait()
    spots = lax.broadcasted_iota(jnp.int32, (blk, ret), 0)
    onehot = (kept_buf[...] == spots).astype(BF16)
    pick = (((0,), (0,)), ((), ()))
    mine[:, :HEAD_DIM] = lax.dot_general(onehot, k_buf[...], pick, preferred_element_type=F32).astype(BF16)
    mine[:, HEAD_DIM:] = lax.dot_general(onehot, v_buf[...], pick, preferred_element_type=F32).astype(BF16)

    first_key = jnp.broadcast_to(k_buf[0:1, :], (ret, HEAD_DIM))
    ones[...] = jnp.ones(ones.shape, BF16)

    def blank(c):
        r = pl.ds(pl.multiple_of(c * ret, ret), ret)
        kv[r, :HEAD_DIM] = first_key
        kv[r, HEAD_DIM:] = jnp.zeros((ret, HEAD_DIM), BF16)
        ones[r, :] = jnp.zeros((ret, HEAD_DIM), BF16)

    loop(y, RING, blank)

    quarter = ANCHOR_TOKENS // RING

    @pl.when(me == 0)
    def _():
        anchor[:, :HEAD_DIM] = k_buf[:ANCHOR_TOKENS, :]
        anchor[:, HEAD_DIM:] = v_buf[:ANCHOR_TOKENS, :]
        kv[RING * ret:RING * ret + quarter, :] = anchor[:quarter, :]

    loads[3].wait()
    lower = lax.broadcasted_iota(jnp.int32, (TILE, TILE), 0) >= lax.broadcasted_iota(jnp.int32, (TILE, TILE), 1)
    lower = jnp.concatenate([lower] * heads, axis=0)
    for c in range(blk // TILE):
        r = slice(c * both, (c + 1) * both)
        for h in range(heads):
            x = q_buf[c * TILE:(c + 1) * TILE, h * HEAD_DIM:(h + 1) * HEAD_DIM].astype(F32) * LOG2_SCALE
            high = x.astype(BF16)
            low = (x - high.astype(F32)).astype(BF16)
            q2_buf[c * both + h * TILE:c * both + (h + 1) * TILE, :] = jnp.concatenate([high, low], axis=1)
        q2 = q2_buf[r, :]
        state = None
        for t in range(c, -1, -1):
            s = scores_of(q2, k_buf[t * TILE:(t + 1) * TILE, :])
            if t == c:
                s = jnp.where(lower, s, NEG)
            state = fold(state, s, v_buf[t * TILE:(t + 1) * TILE, :], jnp.ones((TILE, HEAD_DIM), BF16))
        top[r, :], acc[r, :] = state

    def compute(tiles):
        state = top[...], acc[...]
        for t in tiles:
            r = pl.ds(pl.multiple_of(t * TILE, TILE), TILE)
            state = fold(state, scores_of(q2_buf[...], kv[r, :HEAD_DIM]), kv[r, HEAD_DIM:], ones[r, :])
        top[...], acc[...] = state

    pl.semaphore_wait(barrier, last - z + RING - 1)

    def hand(a):
        return remote(anchor.at[pl.ds(a * quarter, quarter)], slot(RING + a), hand_send.at[a], a_recv.at[0], at(0, a))

    def to_row(c):
        return remote(mine, slot(y), r_send.at[c], r_recv.at[y], at(z, c))

    def from_row(c):
        return remote(mine, slot(c), r_send.at[c], r_recv.at[c], at(z, c))

    def down(t):
        return remote(mine, column_slot(t - 1 - z), z_send.at[t], z_recv.at[t - 1 - z], at(t, y))

    def from_above(i):
        return remote(mine, column_slot(i), z_send.at[0], z_recv.at[i], at(z - 1 - i, y))

    def down_anchor(t):
        return remote(slot(RING + y), slot(RING * (t + 1) + y), a_send.at[t], a_recv.at[0], at(t, y))

    def my_anchor():
        quarter_slot = slot(RING * (z + 1) + y)
        return remote(quarter_slot, quarter_slot, a_send.at[0], a_recv.at[0], at(z, (y + 1) % RING))

    def across(i, d):
        return remote(column_slot(i), cross_slot(i, d), y_send.at[d, i], y_recv.at[d, i], at(z, (y + d) % RING))

    def from_across(i, d):
        return remote(column_slot(i), cross_slot(i, d), y_send.at[d, i], y_recv.at[d, i], at(z, (y + RING - d) % RING))

    def across_anchor(d):
        quarter_slot = slot(RING * (z + 1) + y)
        return remote(quarter_slot, quarter_slot, ay_send.at[d], ay_recv.at[d], at(z, (y + d) % RING))

    def from_across_anchor(d):
        there = (y + RING - d) % RING
        quarter_slot = slot(RING * (z + 1) + there)
        return remote(quarter_slot, quarter_slot, ay_send.at[d], ay_recv.at[d], at(z, there))

    @pl.when(me == 0)
    def _():
        for a in range(1, RING):
            hand(a).start()

    loop(0, last - z, lambda i: down(last - i).start())
    loop(y + 1, RING, lambda c: to_row(c).start())

    @pl.when(z == 0)
    def _():
        @pl.when(y > 0)
        def _():
            my_anchor().wait_recv()

        loop(0, last, lambda i: down_anchor(last - i).start())

    def forward(i):
        from_above(i).wait_recv()
        for d in (2, 1, 3):
            across(i, d).start()

    def forward_anchor():
        @pl.when(z > 0)
        def _():
            my_anchor().wait_recv()

        for d in (2, 1, 3):
            across_anchor(d).start()

    def need(t):
        @pl.when(t == 0)
        def _():
            loop(0, y, lambda c: from_row(c).wait_recv())

        @pl.when((t > 0) & (t <= z))
        def _():
            def one(k):
                u = RING * (t - 1) + k - z

                @pl.when(u >= 0)
                def _():
                    from_across(u // (RING - 1), 1 + u % (RING - 1)).wait_recv()

            loop(0, RING, one)

        @pl.when(t == z + 1)
        def _():
            for d in range(1, RING):
                from_across_anchor(d).wait_recv()

    def pair(p):
        loop(jnp.minimum(z, AHEAD * p), jnp.minimum(z, AHEAD * (p + 1)), forward)

        @pl.when(p == jnp.maximum(z // 2 - 1, 0))
        def _():
            forward_anchor()

        need(2 * p)
        need(2 * p + 1)

        @pl.when(me > 0)
        def _():
            compute([2 * p, 2 * p + 1])

    loop(0, (z + 2) // 2, pair)

    @pl.when(z % 2 == 1)
    def _():
        need(z + 1)
        compute([z + 1])

    for c in range(blk // TILE):
        for h in range(heads):
            r = slice(c * both + h * TILE, c * both + (h + 1) * TILE)
            o_ref[c * TILE:(c + 1) * TILE, h * HEAD_DIM:(h + 1) * HEAD_DIM] = (
                acc[r, :HEAD_DIM] / acc[r, HEAD_DIM:]).astype(BF16)

    def gone(i):
        for d in range(1, RING):
            across(i, d).wait_send()

    loop(0, z, gone)
    for d in range(1, RING):
        across_anchor(d).wait_send()
    loop(y + 1, RING, lambda c: to_row(c).wait_send())
    loop(z + 1, rows, lambda t: down(t).wait_send())

    @pl.when(z == 0)
    def _():
        loop(1, rows, lambda t: down_anchor(t).wait_send())

    @pl.when(me == 0)
    def _():
        for a in range(1, RING):
            hand(a).wait_send()


def on_device(hosts, queries, keys, values, kept):
    blk, width = queries.shape
    heads = width // HEAD_DIM
    ret = kept.shape[2]
    rows = hosts // RING
    hbm = pl.BlockSpec(memory_space=pltpu.HBM)
    dma = pltpu.SemaphoreType.DMA
    return pl.pallas_call(
        functools.partial(kernel, rows, heads),
        out_shape=pltpu.VMEM((blk, width), BF16),
        in_specs=[hbm] * 4,
        out_specs=pl.BlockSpec(memory_space=pltpu.VMEM),
        scratch_shapes=[
            pltpu.VMEM((blk, width), BF16),
            pltpu.VMEM((blk, HEAD_DIM), BF16),
            pltpu.VMEM((blk, HEAD_DIM), BF16),
            pltpu.VMEM((1, ret), jnp.int32),
            pltpu.VMEM((blk * heads, 2 * HEAD_DIM), BF16),
            pltpu.VMEM(((rows + 1) * TILE, 2 * HEAD_DIM), BF16),
            pltpu.VMEM((ANCHOR_TOKENS, 2 * HEAD_DIM), BF16),
            pltpu.VMEM(((rows + 1) * TILE, HEAD_DIM), BF16),
            pltpu.VMEM((ret, 2 * HEAD_DIM), BF16),
            pltpu.VMEM((blk * heads, 2 * HEAD_DIM), F32),
            pltpu.VMEM((blk * heads, HEAD_DIM), F32),
            dma((4,)),
            dma((rows,)), dma((rows,)), dma((RING, rows)), dma((RING, rows)),
            dma((RING,)), dma((RING,)), dma((RING,)),
            dma((1,)), dma((rows,)), dma((RING,)), dma((RING,)),
        ],
        compiler_params=pltpu.CompilerParams(
            collective_id=0, has_side_effects=True, vmem_limit_bytes=61 * 2**20),
    )(queries, keys, values, kept[0])


def solution(mesh):
    placed = (P("ctx", "head"), P("ctx", "head"), P("ctx", "head"), P("head", "ctx", None))
    return jax.shard_map(
        functools.partial(on_device, mesh.shape["ctx"]), mesh=mesh, in_specs=placed,
        out_specs=P("ctx", "head"), check_vma=False)
```

```python
import functools

import jax
import jax.numpy as jnp
from jax import lax
from jax.experimental import pallas as pl
from jax.experimental.pallas import tpu as pltpu
from jax.sharding import PartitionSpec as P

HEAD_DIM = 128
ANCHOR_TOKENS = 256
TILE = 256
AHEAD = 4
NEAR = 2
RING = 4
LOG2_SCALE = HEAD_DIM**-0.5 * 1.4426950408889634
NEG = -1e30
F32, BF16 = jnp.float32, jnp.bfloat16
MESH = pl.DeviceIdType.MESH


def loop(lo, hi, body):
    def step(i, carry):
        body(i)
        return carry

    lax.fori_loop(lo, hi, step, 0)


def scores_of(q2, k):
    k2 = jnp.concatenate([k, k], axis=1)
    return lax.dot_general(q2, k2, (((1,), (1,)), ((), ())), preferred_element_type=F32)


def fold(state, s, v, ones):
    top = jnp.broadcast_to(jnp.max(s, axis=1, keepdims=True), (s.shape[0], HEAD_DIM))
    if state is not None:
        top = jnp.maximum(state[0], top)
    p = jnp.exp2(s - jnp.concatenate([top, top], axis=1)).astype(BF16)
    new = jnp.dot(p, jnp.concatenate([v, ones], axis=1), preferred_element_type=F32)
    if state is not None:
        factor = jnp.exp2(state[0] - top)
        new = state[1] * jnp.concatenate([factor, factor], axis=1) + new
    return top, new


def kernel(rows, heads, q_hbm, k_hbm, v_hbm, kept_hbm, o_ref,
           q_buf, k_buf, v_buf, kept_buf, q2_buf, kv, anchor, ones, mine, other, acc, top,
           in_sem, ready, z_send, z_recv, y_send, y_recv, r_send, r_recv, s_sem, f_send, hand_send, a_recv, a_send, ay_send, ay_recv):
    me = lax.axis_index("ctx")
    z, y = me // RING, me % RING
    blk = k_buf.shape[0]
    ret = mine.shape[0]
    both = heads * TILE
    last = rows - 1

    loads = [pltpu.make_async_copy(a, b, in_sem.at[i]) for i, (a, b) in enumerate(
        [(kept_hbm, kept_buf), (k_hbm, k_buf), (v_hbm, v_buf), (q_hbm, q_buf)])]
    for load in loads:
        load.start()

    def at(zz, yy):
        return {"ctx": zz * RING + yy}

    barrier = pltpu.get_barrier_semaphore()
    loop(1, z, lambda t: pl.semaphore_signal(barrier, inc=1, device_id=at(t, y), device_id_type=MESH))

    @pl.when(z == 0)
    def _():
        loop(1, rows, lambda t: pl.semaphore_signal(barrier, inc=1, device_id=at(t, y), device_id_type=MESH))

    for d in range(1, RING):
        pl.semaphore_signal(barrier, inc=1, device_id=at(z, (y + d) % RING), device_id_type=MESH)

    def slot(n):
        return kv.at[pl.ds(pl.multiple_of(n * ret, ret), ret)]

    def column_slot(i):
        return slot(RING + i)

    def cross_slot(i, d):
        return slot(RING + z + (RING - 1) * i + d - 1)

    def remote(src, dst, send, recv, to):
        return pltpu.make_async_remote_copy(src_ref=src, dst_ref=dst, send_sem=send, recv_sem=recv,
                                            device_id=to, device_id_type=MESH)

    for load in loads[:3]:
        load.wait()
    spots = lax.broadcasted_iota(jnp.int32, (blk, ret), 0)
    onehot = (kept_buf[...] == spots).astype(BF16)
    pick = (((0,), (0,)), ((), ()))
    mine[:, :HEAD_DIM] = lax.dot_general(onehot, k_buf[...], pick, preferred_element_type=F32).astype(BF16)
    mine[:, HEAD_DIM:] = lax.dot_general(onehot, v_buf[...], pick, preferred_element_type=F32).astype(BF16)

    first_key = jnp.broadcast_to(k_buf[0:1, :], (ret, HEAD_DIM))
    ones[...] = jnp.ones(ones.shape, BF16)

    def blank(c):
        r = pl.ds(pl.multiple_of(c * ret, ret), ret)
        kv[r, :HEAD_DIM] = first_key
        kv[r, HEAD_DIM:] = jnp.zeros((ret, HEAD_DIM), BF16)
        ones[r, :] = jnp.zeros((ret, HEAD_DIM), BF16)

    loop(y, RING, blank)

    quarter = ANCHOR_TOKENS // RING

    @pl.when(me == 0)
    def _():
        anchor[:, :HEAD_DIM] = k_buf[:ANCHOR_TOKENS, :]
        anchor[:, HEAD_DIM:] = v_buf[:ANCHOR_TOKENS, :]
        kv[RING * ret:RING * ret + quarter, :] = anchor[:quarter, :]

    def own_block():
        loads[3].wait()
        lower = lax.broadcasted_iota(jnp.int32, (TILE, TILE), 0) >= lax.broadcasted_iota(jnp.int32, (TILE, TILE), 1)
        lower = jnp.concatenate([lower] * heads, axis=0)
        for c in range(blk // TILE):
            r = slice(c * both, (c + 1) * both)
            for h in range(heads):
                x = q_buf[c * TILE:(c + 1) * TILE, h * HEAD_DIM:(h + 1) * HEAD_DIM].astype(F32) * LOG2_SCALE
                high = x.astype(BF16)
                low = (x - high.astype(F32)).astype(BF16)
                q2_buf[c * both + h * TILE:c * both + (h + 1) * TILE, :] = jnp.concatenate([high, low], axis=1)
            q2 = q2_buf[r, :]
            state = None
            for t in range(c, -1, -1):
                s = scores_of(q2, k_buf[t * TILE:(t + 1) * TILE, :])
                if t == c:
                    s = jnp.where(lower, s, NEG)
                state = fold(state, s, v_buf[t * TILE:(t + 1) * TILE, :], jnp.ones((TILE, HEAD_DIM), BF16))
            top[r, :], acc[r, :] = state

    def compute(tiles):
        state = top[...], acc[...]
        for t in tiles:
            r = pl.ds(pl.multiple_of(t * TILE, TILE), TILE)
            state = fold(state, scores_of(q2_buf[...], kv[r, :HEAD_DIM]), kv[r, HEAD_DIM:], ones[r, :])
        top[...], acc[...] = state

    swap = remote(mine, other, s_sem.at[0], s_sem.at[1], at(z, (y + 2) % RING))

    def down_far(i):
        far = slot(RING + z + 1 + i + (RING - 1) * i + 1)
        return remote(other, far, f_send.at[i], y_recv.at[2, i], at(z + 1 + i, y))

    def far_from_above(i):
        return remote(other, cross_slot(i, 2), f_send.at[i], y_recv.at[2, i], at(z - 1 - i, y))

    def hand(a):
        return remote(anchor.at[pl.ds(a * quarter, quarter)], slot(RING + a), hand_send.at[a], a_recv.at[0], at(0, a))

    def to_row(c):
        return remote(mine, slot(y), r_send.at[c], r_recv.at[y], at(z, c))

    def from_row(c):
        return remote(mine, slot(c), r_send.at[c], r_recv.at[c], at(z, c))

    def down(t):
        return remote(mine, column_slot(t - 1 - z), z_send.at[t], z_recv.at[t - 1 - z], at(t, y))

    def from_above(i):
        return remote(mine, column_slot(i), z_send.at[0], z_recv.at[i], at(z - 1 - i, y))

    def down_anchor(t):
        return remote(slot(RING + y), slot(RING * (t + 1) + y), a_send.at[t], a_recv.at[0], at(t, y))

    def my_anchor():
        quarter_slot = slot(RING * (z + 1) + y)
        return remote(quarter_slot, quarter_slot, a_send.at[0], a_recv.at[0], at(z, (y + 1) % RING))

    def across(i, d):
        return remote(column_slot(i), cross_slot(i, d), y_send.at[d, i], y_recv.at[d, i], at(z, (y + d) % RING))

    def from_across(i, d):
        return remote(column_slot(i), cross_slot(i, d), y_send.at[d, i], y_recv.at[d, i], at(z, (y + RING - d) % RING))

    def across_anchor(d):
        quarter_slot = slot(RING * (z + 1) + y)
        return remote(quarter_slot, quarter_slot, ay_send.at[d], ay_recv.at[d], at(z, (y + d) % RING))

    def from_across_anchor(d):
        there = (y + RING - d) % RING
        quarter_slot = slot(RING * (z + 1) + there)
        return remote(quarter_slot, quarter_slot, ay_send.at[d], ay_recv.at[d], at(z, there))

    early = z < rows // 2

    @pl.when(z == 0)
    def _():
        pl.semaphore_wait(barrier, RING - 1)

        @pl.when(y == 0)
        def _():
            for a in range(1, RING):
                hand(a).start()

    @pl.when(early)
    def _():
        own_block()

    @pl.when(z == 0)
    def _():
        @pl.when(y > 0)
        def _():
            my_anchor().wait_recv()

        pl.semaphore_wait(ready, last)

    @pl.when(z > 0)
    def _():
        pl.semaphore_wait(barrier, last - z + RING)
        pl.semaphore_signal(ready, inc=1, device_id=at(0, y), device_id_type=MESH)

    swap.start()
    loop(0, last - z, lambda i: down(last - i).start())

    @pl.when(z == 0)
    def _():
        loop(0, last, lambda i: down_anchor(last - i).start())

    loop(y + 1, RING, lambda c: to_row(c).start())

    @pl.when(jnp.logical_not(early))
    def _():
        own_block()

    swap.wait_recv()
    near = jnp.minimum(NEAR, last - z)
    loop(0, near, lambda i: down_far(i).start())

    def forward(i):
        from_above(i).wait_recv()

        @pl.when(i >= NEAR)
        def _():
            across(i, 2).start()

        for d in (1, 3):
            across(i, d).start()

    def forward_anchor():
        @pl.when(z > 0)
        def _():
            my_anchor().wait_recv()

        for d in (2, 1, 3):
            across_anchor(d).start()

    def need(t):
        @pl.when(t == 0)
        def _():
            loop(0, y, lambda c: from_row(c).wait_recv())

        @pl.when((t > 0) & (t <= z))
        def _():
            def one(k):
                u = RING * (t - 1) + k - z

                @pl.when(u >= 0)
                def _():
                    from_across(u // (RING - 1), 1 + u % (RING - 1)).wait_recv()

            loop(0, RING, one)

        @pl.when(t == z + 1)
        def _():
            for d in range(1, RING):
                from_across_anchor(d).wait_recv()

    def pair(p):
        loop(jnp.minimum(z, AHEAD * p), jnp.minimum(z, AHEAD * (p + 1)), forward)

        @pl.when(p == jnp.minimum(z // 4, 1))
        def _():
            forward_anchor()

        need(2 * p)
        need(2 * p + 1)
        bare = (p == 0) & (y == 0)

        @pl.when(bare & (me > 0))
        def _():
            compute([1])

        @pl.when(jnp.logical_not(bare))
        def _():
            compute([2 * p, 2 * p + 1])

    odd = z % 2
    loop(0, (z + 2 - 3 * odd) // 2, pair)

    @pl.when(z == 1)
    def _():
        forward(0)
        forward_anchor()

    @pl.when(odd == 1)
    def _():
        tiles = [z - 1, z, z + 1]
        for t in tiles:
            need(t)
        compute(tiles)

    for c in range(blk // TILE):
        for h in range(heads):
            r = slice(c * both + h * TILE, c * both + (h + 1) * TILE)
            o_ref[c * TILE:(c + 1) * TILE, h * HEAD_DIM:(h + 1) * HEAD_DIM] = (
                acc[r, :HEAD_DIM] / acc[r, HEAD_DIM:]).astype(BF16)

    def gone(i):
        @pl.when(i >= NEAR)
        def _():
            across(i, 2).wait_send()

        for d in (1, 3):
            across(i, d).wait_send()

    loop(0, z, gone)
    swap.wait_send()
    loop(0, near, lambda i: down_far(i).wait_send())
    for d in range(1, RING):
        across_anchor(d).wait_send()
    loop(y + 1, RING, lambda c: to_row(c).wait_send())
    loop(z + 1, rows, lambda t: down(t).wait_send())

    @pl.when(z == 0)
    def _():
        loop(1, rows, lambda t: down_anchor(t).wait_send())

    @pl.when(me == 0)
    def _():
        for a in range(1, RING):
            hand(a).wait_send()


def on_device(hosts, queries, keys, values, kept):
    blk, width = queries.shape
    heads = width // HEAD_DIM
    ret = kept.shape[2]
    rows = hosts // RING
    hbm = pl.BlockSpec(memory_space=pltpu.HBM)
    dma = pltpu.SemaphoreType.DMA
    return pl.pallas_call(
        functools.partial(kernel, rows, heads),
        out_shape=pltpu.VMEM((blk, width), BF16),
        in_specs=[hbm] * 4,
        out_specs=pl.BlockSpec(memory_space=pltpu.VMEM),
        scratch_shapes=[
            pltpu.VMEM((blk, width), BF16),
            pltpu.VMEM((blk, HEAD_DIM), BF16),
            pltpu.VMEM((blk, HEAD_DIM), BF16),
            pltpu.VMEM((1, ret), jnp.int32),
            pltpu.VMEM((blk * heads, 2 * HEAD_DIM), BF16),
            pltpu.VMEM(((rows + 1) * TILE, 2 * HEAD_DIM), BF16),
            pltpu.VMEM((ANCHOR_TOKENS, 2 * HEAD_DIM), BF16),
            pltpu.VMEM(((rows + 1) * TILE, HEAD_DIM), BF16),
            pltpu.VMEM((ret, 2 * HEAD_DIM), BF16),
            pltpu.VMEM((ret, 2 * HEAD_DIM), BF16),
            pltpu.VMEM((blk * heads, 2 * HEAD_DIM), F32),
            pltpu.VMEM((blk * heads, HEAD_DIM), F32),
            dma((4,)),
            pltpu.SemaphoreType.REGULAR,
            dma((rows,)), dma((rows,)), dma((RING, rows)), dma((RING, rows)),
            dma((RING,)), dma((RING,)), dma((2,)), dma((NEAR,)), dma((RING,)),
            dma((1,)), dma((rows,)), dma((RING,)), dma((RING,)),
        ],
        compiler_params=pltpu.CompilerParams(
            collective_id=0, has_side_effects=True, vmem_limit_bytes=61 * 2**20),
    )(queries, keys, values, kept[0])


def solution(mesh):
    placed = (P("ctx", "head"), P("ctx", "head"), P("ctx", "head"), P("head", "ctx", None))
    return jax.shard_map(
        functools.partial(on_device, mesh.shape["ctx"]), mesh=mesh, in_specs=placed,
        out_specs=P("ctx", "head"), check_vma=False)
```

```python
import functools

import jax
import jax.numpy as jnp
from jax import lax
from jax.experimental import pallas as pl
from jax.experimental.pallas import tpu as pltpu
from jax.sharding import PartitionSpec as P

HEAD_DIM = 128
ANCHOR_TOKENS = 256
TILE = 256
AHEAD = 4
NEAR = 1
RING = 4
LOG2_SCALE = HEAD_DIM**-0.5 * 1.4426950408889634
NEG = -1e30
F32, BF16 = jnp.float32, jnp.bfloat16
MESH = pl.DeviceIdType.MESH


def loop(lo, hi, body):
    def step(i, carry):
        body(i)
        return carry

    lax.fori_loop(lo, hi, step, 0)


def scores_of(q2, k):
    k2 = jnp.concatenate([k, k], axis=1)
    return lax.dot_general(q2, k2, (((1,), (1,)), ((), ())), preferred_element_type=F32)


def fold(state, s, v, ones):
    top = jnp.broadcast_to(jnp.max(s, axis=1, keepdims=True), (s.shape[0], HEAD_DIM))
    if state is not None:
        top = jnp.maximum(state[0], top)
    p = jnp.exp2(s - jnp.concatenate([top, top], axis=1)).astype(BF16)
    new = jnp.dot(p, jnp.concatenate([v, ones], axis=1), preferred_element_type=F32)
    if state is not None:
        factor = jnp.exp2(state[0] - top)
        new = state[1] * jnp.concatenate([factor, factor], axis=1) + new
    return top, new


def kernel(rows, heads, q_hbm, k_hbm, v_hbm, kept_hbm, o_ref,
           q_buf, k_buf, v_buf, kept_buf, q2_buf, kv, anchor, ones, mine, other, acc, top,
           in_sem, ready, z_send, z_recv, y_send, y_recv, r_send, r_recv, s_sem, f_send, hand_send, a_recv, a_send, ay_send, ay_recv):
    me = lax.axis_index("ctx")
    z, y = me // RING, me % RING
    blk = k_buf.shape[0]
    ret = mine.shape[0]
    both = heads * TILE
    last = rows - 1

    loads = [pltpu.make_async_copy(a, b, in_sem.at[i]) for i, (a, b) in enumerate(
        [(kept_hbm, kept_buf), (k_hbm, k_buf), (v_hbm, v_buf), (q_hbm, q_buf)])]
    for load in loads:
        load.start()

    def at(zz, yy):
        return {"ctx": zz * RING + yy}

    barrier = pltpu.get_barrier_semaphore()
    loop(1, z, lambda t: pl.semaphore_signal(barrier, inc=1, device_id=at(t, y), device_id_type=MESH))

    @pl.when(z == 0)
    def _():
        loop(1, rows, lambda t: pl.semaphore_signal(barrier, inc=1, device_id=at(t, y), device_id_type=MESH))

    for d in range(1, RING):
        pl.semaphore_signal(barrier, inc=1, device_id=at(z, (y + d) % RING), device_id_type=MESH)

    def slot(n):
        return kv.at[pl.ds(pl.multiple_of(n * ret, ret), ret)]

    def column_slot(i):
        return slot(RING + i)

    def cross_slot(i, d):
        return slot(RING + z + (RING - 1) * i + d - 1)

    def remote(src, dst, send, recv, to):
        return pltpu.make_async_remote_copy(src_ref=src, dst_ref=dst, send_sem=send, recv_sem=recv,
                                            device_id=to, device_id_type=MESH)

    for load in loads[:3]:
        load.wait()
    spots = lax.broadcasted_iota(jnp.int32, (blk, ret), 0)
    onehot = (kept_buf[...] == spots).astype(BF16)
    pick = (((0,), (0,)), ((), ()))
    mine[:, :HEAD_DIM] = lax.dot_general(onehot, k_buf[...], pick, preferred_element_type=F32).astype(BF16)
    mine[:, HEAD_DIM:] = lax.dot_general(onehot, v_buf[...], pick, preferred_element_type=F32).astype(BF16)

    first_key = jnp.broadcast_to(k_buf[0:1, :], (ret, HEAD_DIM))
    ones[...] = jnp.ones(ones.shape, BF16)

    def blank(c):
        r = pl.ds(pl.multiple_of(c * ret, ret), ret)
        kv[r, :HEAD_DIM] = first_key
        kv[r, HEAD_DIM:] = jnp.zeros((ret, HEAD_DIM), BF16)
        ones[r, :] = jnp.zeros((ret, HEAD_DIM), BF16)

    loop(y, RING, blank)

    quarter = ANCHOR_TOKENS // RING

    @pl.when(me == 0)
    def _():
        anchor[:, :HEAD_DIM] = k_buf[:ANCHOR_TOKENS, :]
        anchor[:, HEAD_DIM:] = v_buf[:ANCHOR_TOKENS, :]
        kv[RING * ret:RING * ret + quarter, :] = anchor[:quarter, :]

    def own_block():
        loads[3].wait()
        lower = lax.broadcasted_iota(jnp.int32, (TILE, TILE), 0) >= lax.broadcasted_iota(jnp.int32, (TILE, TILE), 1)
        lower = jnp.concatenate([lower] * heads, axis=0)
        for c in range(blk // TILE):
            r = slice(c * both, (c + 1) * both)
            for h in range(heads):
                x = q_buf[c * TILE:(c + 1) * TILE, h * HEAD_DIM:(h + 1) * HEAD_DIM].astype(F32) * LOG2_SCALE
                high = x.astype(BF16)
                low = (x - high.astype(F32)).astype(BF16)
                q2_buf[c * both + h * TILE:c * both + (h + 1) * TILE, :] = jnp.concatenate([high, low], axis=1)
            q2 = q2_buf[r, :]
            state = None
            for t in range(c, -1, -1):
                s = scores_of(q2, k_buf[t * TILE:(t + 1) * TILE, :])
                if t == c:
                    s = jnp.where(lower, s, NEG)
                state = fold(state, s, v_buf[t * TILE:(t + 1) * TILE, :], jnp.ones((TILE, HEAD_DIM), BF16))
            top[r, :], acc[r, :] = state

    def compute(t):
        r = pl.ds(pl.multiple_of(t * TILE, TILE), TILE)
        s = scores_of(q2_buf[...], kv[r, :HEAD_DIM])
        top[...], acc[...] = fold((top[...], acc[...]), s, kv[r, HEAD_DIM:], ones[r, :])

    swap = remote(mine, other, s_sem.at[0], s_sem.at[1], at(z, (y + 2) % RING))

    def down_far(i):
        far = slot(RING + z + 1 + i + (RING - 1) * i + 1)
        return remote(other, far, f_send.at[i], y_recv.at[2, i], at(z + 1 + i, y))

    def far_from_above(i):
        return remote(other, cross_slot(i, 2), f_send.at[i], y_recv.at[2, i], at(z - 1 - i, y))

    def hand(a):
        return remote(anchor.at[pl.ds(a * quarter, quarter)], slot(RING + a), hand_send.at[a], a_recv.at[0], at(0, a))

    def to_row(c):
        return remote(mine, slot(y), r_send.at[c], r_recv.at[y], at(z, c))

    def from_row(c):
        return remote(mine, slot(c), r_send.at[c], r_recv.at[c], at(z, c))

    def down(t):
        return remote(mine, column_slot(t - 1 - z), z_send.at[t], z_recv.at[t - 1 - z], at(t, y))

    def from_above(i):
        return remote(mine, column_slot(i), z_send.at[0], z_recv.at[i], at(z - 1 - i, y))

    def down_anchor(t):
        return remote(slot(RING + y), slot(RING * (t + 1) + y), a_send.at[t], a_recv.at[0], at(t, y))

    def my_anchor():
        quarter_slot = slot(RING * (z + 1) + y)
        return remote(quarter_slot, quarter_slot, a_send.at[0], a_recv.at[0], at(z, (y + 1) % RING))

    def across(i, d):
        return remote(column_slot(i), cross_slot(i, d), y_send.at[d, i], y_recv.at[d, i], at(z, (y + d) % RING))

    def from_across(i, d):
        return remote(column_slot(i), cross_slot(i, d), y_send.at[d, i], y_recv.at[d, i], at(z, (y + RING - d) % RING))

    def across_anchor(d):
        quarter_slot = slot(RING * (z + 1) + y)
        return remote(quarter_slot, quarter_slot, ay_send.at[d], ay_recv.at[d], at(z, (y + d) % RING))

    def from_across_anchor(d):
        there = (y + RING - d) % RING
        quarter_slot = slot(RING * (z + 1) + there)
        return remote(quarter_slot, quarter_slot, ay_send.at[d], ay_recv.at[d], at(z, there))

    early = z < rows // 2

    @pl.when(z == 0)
    def _():
        pl.semaphore_wait(barrier, RING - 1)

        @pl.when(y == 0)
        def _():
            for a in range(1, RING):
                hand(a).start()

    @pl.when(early)
    def _():
        own_block()

    @pl.when(z == 0)
    def _():
        @pl.when(y > 0)
        def _():
            my_anchor().wait_recv()

        pl.semaphore_wait(ready, last)

    @pl.when(z > 0)
    def _():
        pl.semaphore_wait(barrier, last - z + RING)
        pl.semaphore_signal(ready, inc=1, device_id=at(0, y), device_id_type=MESH)

    swap.start()
    mid = rows // 2
    for t in [last, mid - 1] + [t for t in range(last - 1, 0, -1) if t != mid - 1]:
        @pl.when(z < t)
        def _():
            down(t).start()


    @pl.when(z == 0)
    def _():
        loop(0, last, lambda i: down_anchor(last - i).start())

    loop(y + 1, RING, lambda c: to_row(c).start())

    @pl.when(jnp.logical_not(early))
    def _():
        own_block()

    swap.wait_recv()
    near = jnp.minimum(NEAR, last - z)
    loop(0, near, lambda i: down_far(i).start())

    def forward(i):
        from_above(i).wait_recv()

        @pl.when(i >= NEAR)
        def _():
            across(i, 2).start()

        for d in (1, 3):
            across(i, d).start()

    def forward_anchor():
        @pl.when(z > 0)
        def _():
            my_anchor().wait_recv()

        for d in (2, 1, 3):
            across_anchor(d).start()

    def need(t):
        @pl.when(t == 0)
        def _():
            loop(0, y, lambda c: from_row(c).wait_recv())

        @pl.when((t > 0) & (t <= z))
        def _():
            def one(k):
                u = RING * (t - 1) + k - z

                @pl.when(u >= 0)
                def _():
                    from_across(u // (RING - 1), 1 + u % (RING - 1)).wait_recv()

            loop(0, RING, one)

        @pl.when(t == z + 1)
        def _():
            for d in range(1, RING):
                from_across_anchor(d).wait_recv()

    low = z // (rows // 2)

    def step(k):
        late = (k + rows - z) // rows
        tile = k + low * late * (1 - 2 * (k - z))

        @pl.when(k > 0)
        def _():
            loop(jnp.minimum(z, AHEAD * (k - 1)), jnp.minimum(z, AHEAD * k), forward)

        @pl.when(k == 1 + 2 * low)
        def _():
            forward_anchor()

        need(tile)

        @pl.when((me > 0) & (k + y > 0))
        def _():
            compute(tile)

    loop(0, z + 2, step)

    for c in range(blk // TILE):
        for h in range(heads):
            r = slice(c * both + h * TILE, c * both + (h + 1) * TILE)
            o_ref[c * TILE:(c + 1) * TILE, h * HEAD_DIM:(h + 1) * HEAD_DIM] = (
                acc[r, :HEAD_DIM] / acc[r, HEAD_DIM:]).astype(BF16)

    def gone(i):
        @pl.when(i >= NEAR)
        def _():
            across(i, 2).wait_send()

        for d in (1, 3):
            across(i, d).wait_send()

    loop(0, z, gone)
    swap.wait_send()
    loop(0, near, lambda i: down_far(i).wait_send())
    for d in range(1, RING):
        across_anchor(d).wait_send()
    loop(y + 1, RING, lambda c: to_row(c).wait_send())
    loop(z + 1, rows, lambda t: down(t).wait_send())

    @pl.when(z == 0)
    def _():
        loop(1, rows, lambda t: down_anchor(t).wait_send())

    @pl.when(me == 0)
    def _():
        for a in range(1, RING):
            hand(a).wait_send()


def on_device(hosts, queries, keys, values, kept):
    blk, width = queries.shape
    heads = width // HEAD_DIM
    ret = kept.shape[2]
    rows = hosts // RING
    hbm = pl.BlockSpec(memory_space=pltpu.HBM)
    dma = pltpu.SemaphoreType.DMA
    return pl.pallas_call(
        functools.partial(kernel, rows, heads),
        out_shape=pltpu.VMEM((blk, width), BF16),
        in_specs=[hbm] * 4,
        out_specs=pl.BlockSpec(memory_space=pltpu.VMEM),
        scratch_shapes=[
            pltpu.VMEM((blk, width), BF16),
            pltpu.VMEM((blk, HEAD_DIM), BF16),
            pltpu.VMEM((blk, HEAD_DIM), BF16),
            pltpu.VMEM((1, ret), jnp.int32),
            pltpu.VMEM((blk * heads, 2 * HEAD_DIM), BF16),
            pltpu.VMEM(((rows + 1) * TILE, 2 * HEAD_DIM), BF16),
            pltpu.VMEM((ANCHOR_TOKENS, 2 * HEAD_DIM), BF16),
            pltpu.VMEM(((rows + 1) * TILE, HEAD_DIM), BF16),
            pltpu.VMEM((ret, 2 * HEAD_DIM), BF16),
            pltpu.VMEM((ret, 2 * HEAD_DIM), BF16),
            pltpu.VMEM((blk * heads, 2 * HEAD_DIM), F32),
            pltpu.VMEM((blk * heads, HEAD_DIM), F32),
            dma((4,)),
            pltpu.SemaphoreType.REGULAR,
            dma((rows,)), dma((rows,)), dma((RING, rows)), dma((RING, rows)),
            dma((RING,)), dma((RING,)), dma((2,)), dma((NEAR,)), dma((RING,)),
            dma((1,)), dma((rows,)), dma((RING,)), dma((RING,)),
        ],
        compiler_params=pltpu.CompilerParams(
            collective_id=0, has_side_effects=True, vmem_limit_bytes=61 * 2**20),
    )(queries, keys, values, kept[0])


def solution(mesh):
    placed = (P("ctx", "head"), P("ctx", "head"), P("ctx", "head"), P("head", "ctx", None))
    return jax.shard_map(
        functools.partial(on_device, mesh.shape["ctx"]), mesh=mesh, in_specs=placed,
        out_specs=P("ctx", "head"), check_vma=False)
```

```python
import functools

import jax
import jax.numpy as jnp
from jax import lax
from jax.experimental import pallas as pl
from jax.experimental.pallas import tpu as pltpu
from jax.sharding import PartitionSpec as P

HEAD_DIM = 128
ANCHOR_TOKENS = 256
TILE = 256
AHEAD = 4
NEAR = 2
RING = 4
LOG2_SCALE = HEAD_DIM**-0.5 * 1.4426950408889634
NEG = -1e30
F32, BF16 = jnp.float32, jnp.bfloat16
MESH = pl.DeviceIdType.MESH


def loop(lo, hi, body):
    def step(i, carry):
        body(i)
        return carry

    lax.fori_loop(lo, hi, step, 0)


def scores_of(q2, k):
    k2 = jnp.concatenate([k, k], axis=1)
    return lax.dot_general(q2, k2, (((1,), (1,)), ((), ())), preferred_element_type=F32)


def fold(state, s, v, ones):
    top = jnp.broadcast_to(jnp.max(s, axis=1, keepdims=True), (s.shape[0], HEAD_DIM))
    if state is not None:
        top = jnp.maximum(state[0], top)
    p = jnp.exp2(s - jnp.concatenate([top, top], axis=1)).astype(BF16)
    new = jnp.dot(p, jnp.concatenate([v, ones], axis=1), preferred_element_type=F32)
    if state is not None:
        factor = jnp.exp2(state[0] - top)
        new = state[1] * jnp.concatenate([factor, factor], axis=1) + new
    return top, new


def kernel(rows, heads, q_hbm, k_hbm, v_hbm, kept_hbm, o_ref,
           q_buf, k_buf, v_buf, kept_buf, q2_buf, kv, anchor, ones, mine, other, acc, top,
           in_sem, ready, z_send, z_recv, y_send, y_recv, r_send, r_recv, s_sem, f_send, hand_send, a_recv, a_send, ay_send, ay_recv):
    me = lax.axis_index("ctx")
    z, y = me // RING, me % RING
    blk = k_buf.shape[0]
    ret = mine.shape[0]
    both = heads * TILE
    last = rows - 1

    loads = [pltpu.make_async_copy(a, b, in_sem.at[i]) for i, (a, b) in enumerate(
        [(kept_hbm, kept_buf), (k_hbm, k_buf), (v_hbm, v_buf), (q_hbm, q_buf)])]
    for load in loads:
        load.start()

    def at(zz, yy):
        return {"ctx": zz * RING + yy}

    barrier = pltpu.get_barrier_semaphore()
    loop(1, z, lambda t: pl.semaphore_signal(barrier, inc=1, device_id=at(t, y), device_id_type=MESH))

    @pl.when(z == 0)
    def _():
        loop(1, rows, lambda t: pl.semaphore_signal(barrier, inc=1, device_id=at(t, y), device_id_type=MESH))

    for d in range(1, RING):
        pl.semaphore_signal(barrier, inc=1, device_id=at(z, (y + d) % RING), device_id_type=MESH)

    def slot(n):
        return kv.at[pl.ds(pl.multiple_of(n * ret, ret), ret)]

    def column_slot(i):
        return slot(RING + i)

    def cross_slot(i, d):
        return slot(RING + z + (RING - 1) * i + d - 1)

    def remote(src, dst, send, recv, to):
        return pltpu.make_async_remote_copy(src_ref=src, dst_ref=dst, send_sem=send, recv_sem=recv,
                                            device_id=to, device_id_type=MESH)

    for load in loads[:3]:
        load.wait()
    spots = lax.broadcasted_iota(jnp.int32, (blk, ret), 0)
    onehot = (kept_buf[...] == spots).astype(BF16)
    pick = (((0,), (0,)), ((), ()))
    mine[:, :HEAD_DIM] = lax.dot_general(onehot, k_buf[...], pick, preferred_element_type=F32).astype(BF16)
    mine[:, HEAD_DIM:] = lax.dot_general(onehot, v_buf[...], pick, preferred_element_type=F32).astype(BF16)

    first_key = jnp.broadcast_to(k_buf[0:1, :], (ret, HEAD_DIM))
    ones[...] = jnp.ones(ones.shape, BF16)

    def blank(c):
        r = pl.ds(pl.multiple_of(c * ret, ret), ret)
        kv[r, :HEAD_DIM] = first_key
        kv[r, HEAD_DIM:] = jnp.zeros((ret, HEAD_DIM), BF16)
        ones[r, :] = jnp.zeros((ret, HEAD_DIM), BF16)

    loop(y, RING, blank)

    quarter = ANCHOR_TOKENS // RING

    @pl.when(me == 0)
    def _():
        anchor[:, :HEAD_DIM] = k_buf[:ANCHOR_TOKENS, :]
        anchor[:, HEAD_DIM:] = v_buf[:ANCHOR_TOKENS, :]
        kv[RING * ret:RING * ret + quarter, :] = anchor[:quarter, :]

    def own_block():
        loads[3].wait()
        lower = lax.broadcasted_iota(jnp.int32, (TILE, TILE), 0) >= lax.broadcasted_iota(jnp.int32, (TILE, TILE), 1)
        lower = jnp.concatenate([lower] * heads, axis=0)
        for c in range(blk // TILE):
            r = slice(c * both, (c + 1) * both)
            for h in range(heads):
                x = q_buf[c * TILE:(c + 1) * TILE, h * HEAD_DIM:(h + 1) * HEAD_DIM].astype(F32) * LOG2_SCALE
                high = x.astype(BF16)
                low = (x - high.astype(F32)).astype(BF16)
                q2_buf[c * both + h * TILE:c * both + (h + 1) * TILE, :] = jnp.concatenate([high, low], axis=1)
            q2 = q2_buf[r, :]
            state = None
            for t in range(c, -1, -1):
                s = scores_of(q2, k_buf[t * TILE:(t + 1) * TILE, :])
                if t == c:
                    s = jnp.where(lower, s, NEG)
                state = fold(state, s, v_buf[t * TILE:(t + 1) * TILE, :], jnp.ones((TILE, HEAD_DIM), BF16))
            top[r, :], acc[r, :] = state

    def folded(t):
        r = pl.ds(pl.multiple_of(t * TILE, TILE), TILE)
        s = scores_of(q2_buf[...], kv[r, :HEAD_DIM])
        return fold((top[...], acc[...]), s, kv[r, HEAD_DIM:], ones[r, :])

    def compute(t):
        top[...], acc[...] = folded(t)

    def finish(total):
        for c in range(blk // TILE):
            for h in range(heads):
                r = slice(c * both + h * TILE, c * both + (h + 1) * TILE)
                o_ref[c * TILE:(c + 1) * TILE, h * HEAD_DIM:(h + 1) * HEAD_DIM] = (
                    total[r, :HEAD_DIM] / total[r, HEAD_DIM:]).astype(BF16)

    swap = remote(mine, other, s_sem.at[0], s_sem.at[1], at(z, (y + 2) % RING))

    def down_far(i):
        far = slot(RING + z + 1 + i + (RING - 1) * i + 1)
        return remote(other, far, f_send.at[i], y_recv.at[2, i], at(z + 1 + i, y))

    def far_from_above(i):
        return remote(other, cross_slot(i, 2), f_send.at[i], y_recv.at[2, i], at(z - 1 - i, y))

    def hand(a):
        return remote(anchor.at[pl.ds(a * quarter, quarter)], slot(RING + a), hand_send.at[a], a_recv.at[0], at(0, a))

    def to_row(c):
        return remote(mine, slot(y), r_send.at[c], r_recv.at[y], at(z, c))

    def from_row(c):
        return remote(mine, slot(c), r_send.at[c], r_recv.at[c], at(z, c))

    def down(t):
        return remote(mine, column_slot(t - 1 - z), z_send.at[t], z_recv.at[t - 1 - z], at(t, y))

    def from_above(i):
        return remote(mine, column_slot(i), z_send.at[0], z_recv.at[i], at(z - 1 - i, y))

    def down_anchor(t):
        return remote(slot(RING + y), slot(RING * (t + 1) + y), a_send.at[t], a_recv.at[0], at(t, y))

    def my_anchor():
        quarter_slot = slot(RING * (z + 1) + y)
        return remote(quarter_slot, quarter_slot, a_send.at[0], a_recv.at[0], at(z, (y + 1) % RING))

    def across(i, d):
        return remote(column_slot(i), cross_slot(i, d), y_send.at[d, i], y_recv.at[d, i], at(z, (y + d) % RING))

    def from_across(i, d):
        return remote(column_slot(i), cross_slot(i, d), y_send.at[d, i], y_recv.at[d, i], at(z, (y + RING - d) % RING))

    def across_anchor(d):
        quarter_slot = slot(RING * (z + 1) + y)
        return remote(quarter_slot, quarter_slot, ay_send.at[d], ay_recv.at[d], at(z, (y + d) % RING))

    def from_across_anchor(d):
        there = (y + RING - d) % RING
        quarter_slot = slot(RING * (z + 1) + there)
        return remote(quarter_slot, quarter_slot, ay_send.at[d], ay_recv.at[d], at(z, there))

    early = z < rows // 2

    @pl.when(z == 0)
    def _():
        pl.semaphore_wait(barrier, RING - 1)

        @pl.when(y == 0)
        def _():
            for a in range(1, RING):
                hand(a).start()

    @pl.when(early)
    def _():
        own_block()

    @pl.when(z == 0)
    def _():
        @pl.when(y > 0)
        def _():
            my_anchor().wait_recv()

        pl.semaphore_wait(ready, last)

    @pl.when(z > 0)
    def _():
        pl.semaphore_wait(barrier, last - z + RING)
        pl.semaphore_signal(ready, inc=1, device_id=at(0, y), device_id_type=MESH)

    swap.start()
    loop(0, last - z, lambda i: down(last - i).start())

    @pl.when(z == 0)
    def _():
        loop(0, last, lambda i: down_anchor(last - i).start())

    loop(y + 1, RING, lambda c: to_row(c).start())

    @pl.when(jnp.logical_not(early))
    def _():
        own_block()

    swap.wait_recv()
    doubled = 1 + (NEAR - 1) * (z // last)

    def each_far(go):
        @pl.when(z < last)
        def _():
            go(down_far(0))

        for i in range(1, NEAR):
            @pl.when(z + 1 + i == last)
            def _():
                go(down_far(i))

    each_far(lambda copy: copy.start())

    def forward(i):
        from_above(i).wait_recv()

        @pl.when(i >= doubled)
        def _():
            across(i, 2).start()

        for d in (1, 3):
            across(i, d).start()

    def forward_anchor():
        @pl.when(z > 0)
        def _():
            my_anchor().wait_recv()

        for d in (2, 1, 3):
            across_anchor(d).start()

    def need(t):
        @pl.when(t == 0)
        def _():
            loop(0, y, lambda c: from_row(c).wait_recv())

        @pl.when((t > 0) & (t <= z))
        def _():
            def one(k):
                u = RING * (t - 1) + k - z

                @pl.when(u >= 0)
                def _():
                    from_across(u // (RING - 1), 1 + u % (RING - 1)).wait_recv()

            loop(0, RING, one)

        @pl.when(t == z + 1)
        def _():
            for d in range(1, RING):
                from_across_anchor(d).wait_recv()

    low = z // (rows // 2)

    def step(k):
        late = (k + rows - z) // rows
        tile = k + low * late * (1 - 2 * (k - z))

        @pl.when(k > 0)
        def _():
            loop(jnp.minimum(z, AHEAD * (k - 1)), jnp.minimum(z, AHEAD * k), forward)

        @pl.when(k == 1 + 2 * low)
        def _():
            forward_anchor()

        need(tile)
        return tile

    def work(k):
        tile = step(k)

        @pl.when((me > 0) & (k + y > 0))
        def _():
            compute(tile)

    loop(0, z + 1, work)
    final = step(z + 1)

    @pl.when(me > 0)
    def _():
        finish(folded(final)[1])

    @pl.when(me == 0)
    def _():
        finish(acc[...])

    def gone(i):
        @pl.when(i >= doubled)
        def _():
            across(i, 2).wait_send()

        for d in (1, 3):
            across(i, d).wait_send()

    loop(0, z, gone)
    swap.wait_send()
    each_far(lambda copy: copy.wait_send())
    for d in range(1, RING):
        across_anchor(d).wait_send()
    loop(y + 1, RING, lambda c: to_row(c).wait_send())
    loop(z + 1, rows, lambda t: down(t).wait_send())

    @pl.when(z == 0)
    def _():
        loop(1, rows, lambda t: down_anchor(t).wait_send())

    @pl.when(me == 0)
    def _():
        for a in range(1, RING):
            hand(a).wait_send()


def on_device(hosts, queries, keys, values, kept):
    blk, width = queries.shape
    heads = width // HEAD_DIM
    ret = kept.shape[2]
    rows = hosts // RING
    hbm = pl.BlockSpec(memory_space=pltpu.HBM)
    dma = pltpu.SemaphoreType.DMA
    return pl.pallas_call(
        functools.partial(kernel, rows, heads),
        out_shape=pltpu.VMEM((blk, width), BF16),
        in_specs=[hbm] * 4,
        out_specs=pl.BlockSpec(memory_space=pltpu.VMEM),
        scratch_shapes=[
            pltpu.VMEM((blk, width), BF16),
            pltpu.VMEM((blk, HEAD_DIM), BF16),
            pltpu.VMEM((blk, HEAD_DIM), BF16),
            pltpu.VMEM((1, ret), jnp.int32),
            pltpu.VMEM((blk * heads, 2 * HEAD_DIM), BF16),
            pltpu.VMEM(((rows + 1) * TILE, 2 * HEAD_DIM), BF16),
            pltpu.VMEM((ANCHOR_TOKENS, 2 * HEAD_DIM), BF16),
            pltpu.VMEM(((rows + 1) * TILE, HEAD_DIM), BF16),
            pltpu.VMEM((ret, 2 * HEAD_DIM), BF16),
            pltpu.VMEM((ret, 2 * HEAD_DIM), BF16),
            pltpu.VMEM((blk * heads, 2 * HEAD_DIM), F32),
            pltpu.VMEM((blk * heads, HEAD_DIM), F32),
            dma((4,)),
            pltpu.SemaphoreType.REGULAR,
            dma((rows,)), dma((rows,)), dma((RING, rows)), dma((RING, rows)),
            dma((RING,)), dma((RING,)), dma((2,)), dma((NEAR,)), dma((RING,)),
            dma((1,)), dma((rows,)), dma((RING,)), dma((RING,)),
        ],
        compiler_params=pltpu.CompilerParams(
            collective_id=0, has_side_effects=True, vmem_limit_bytes=61 * 2**20),
    )(queries, keys, values, kept[0])


def solution(mesh):
    placed = (P("ctx", "head"), P("ctx", "head"), P("ctx", "head"), P("head", "ctx", None))
    return jax.shard_map(
        functools.partial(on_device, mesh.shape["ctx"]), mesh=mesh, in_specs=placed,
        out_specs=P("ctx", "head"), check_vma=False)
```

```python
import functools

import jax
import jax.numpy as jnp
from jax import lax
from jax.experimental import pallas as pl
from jax.experimental.pallas import tpu as pltpu
from jax.sharding import PartitionSpec as P

HEAD_DIM = 128
ANCHOR_TOKENS = 256
TILE = 256
AHEAD = 4
NEAR = 2
RING = 4
LOG2_SCALE = HEAD_DIM**-0.5 * 1.4426950408889634
NEG = -1e30
F32, BF16 = jnp.float32, jnp.bfloat16
MESH = pl.DeviceIdType.MESH


def loop(lo, hi, body):
    def step(i, carry):
        body(i)
        return carry

    lax.fori_loop(lo, hi, step, 0)


def scores_of(q2, k):
    k2 = jnp.concatenate([k, k], axis=1)
    return lax.dot_general(q2, k2, (((1,), (1,)), ((), ())), preferred_element_type=F32)


def fold(state, s, v, ones):
    top = jnp.broadcast_to(jnp.max(s, axis=1, keepdims=True), (s.shape[0], HEAD_DIM))
    if state is not None:
        top = jnp.maximum(state[0], top)
    p = jnp.exp2(s - jnp.concatenate([top, top], axis=1)).astype(BF16)
    new = jnp.dot(p, jnp.concatenate([v, ones], axis=1), preferred_element_type=F32)
    if state is not None:
        factor = jnp.exp2(state[0] - top)
        new = state[1] * jnp.concatenate([factor, factor], axis=1) + new
    return top, new


def kernel(rows, heads, q_hbm, k_hbm, v_hbm, kept_hbm, o_ref,
           q_buf, k_buf, v_buf, kept_buf, q2_buf, kv, anchor, ones, mine, other, acc, top,
           in_sem, ready, z_send, z_recv, y_send, y_recv, r_send, r_recv, s_sem, f_send, hand_send, a_recv, a_send, ay_send, ay_recv):
    me = lax.axis_index("ctx")
    z, y = me // RING, me % RING
    blk = k_buf.shape[0]
    ret = mine.shape[0]
    both = heads * TILE
    last = rows - 1

    loads = [pltpu.make_async_copy(a, b, in_sem.at[i]) for i, (a, b) in enumerate(
        [(kept_hbm, kept_buf), (k_hbm, k_buf), (v_hbm, v_buf), (q_hbm, q_buf)])]
    for load in loads:
        load.start()

    def at(zz, yy):
        return {"ctx": zz * RING + yy}

    barrier = pltpu.get_barrier_semaphore()
    loop(1, z, lambda t: pl.semaphore_signal(barrier, inc=1, device_id=at(t, y), device_id_type=MESH))

    @pl.when(z == 0)
    def _():
        loop(1, rows, lambda t: pl.semaphore_signal(barrier, inc=1, device_id=at(t, y), device_id_type=MESH))

    for d in range(1, RING):
        pl.semaphore_signal(barrier, inc=1, device_id=at(z, (y + d) % RING), device_id_type=MESH)

    def slot(n):
        return kv.at[pl.ds(pl.multiple_of(n * ret, ret), ret)]

    def column_slot(i):
        return slot(RING + i)

    def cross_slot(i, d):
        return slot(RING + z + (RING - 1) * i + d - 1)

    def remote(src, dst, send, recv, to):
        return pltpu.make_async_remote_copy(src_ref=src, dst_ref=dst, send_sem=send, recv_sem=recv,
                                            device_id=to, device_id_type=MESH)

    for load in loads[:3]:
        load.wait()
    spots = lax.broadcasted_iota(jnp.int32, (blk, ret), 0)
    onehot = (kept_buf[...] == spots).astype(BF16)
    pick = (((0,), (0,)), ((), ()))
    mine[:, :HEAD_DIM] = lax.dot_general(onehot, k_buf[...], pick, preferred_element_type=F32).astype(BF16)
    mine[:, HEAD_DIM:] = lax.dot_general(onehot, v_buf[...], pick, preferred_element_type=F32).astype(BF16)

    first_key = jnp.broadcast_to(k_buf[0:1, :], (ret, HEAD_DIM))
    ones[...] = jnp.ones(ones.shape, BF16)

    def blank(c):
        r = pl.ds(pl.multiple_of(c * ret, ret), ret)
        kv[r, :HEAD_DIM] = first_key
        kv[r, HEAD_DIM:] = jnp.zeros((ret, HEAD_DIM), BF16)
        ones[r, :] = jnp.zeros((ret, HEAD_DIM), BF16)

    loop(y, RING, blank)

    quarter = ANCHOR_TOKENS // RING

    @pl.when(me == 0)
    def _():
        anchor[:, :HEAD_DIM] = k_buf[:ANCHOR_TOKENS, :]
        anchor[:, HEAD_DIM:] = v_buf[:ANCHOR_TOKENS, :]
        kv[RING * ret:RING * ret + quarter, :] = anchor[:quarter, :]

    def own_block():
        loads[3].wait()
        lower = lax.broadcasted_iota(jnp.int32, (TILE, TILE), 0) >= lax.broadcasted_iota(jnp.int32, (TILE, TILE), 1)
        lower = jnp.concatenate([lower] * heads, axis=0)
        for c in range(blk // TILE):
            r = slice(c * both, (c + 1) * both)
            for h in range(heads):
                x = q_buf[c * TILE:(c + 1) * TILE, h * HEAD_DIM:(h + 1) * HEAD_DIM].astype(F32) * LOG2_SCALE
                high = x.astype(BF16)
                low = (x - high.astype(F32)).astype(BF16)
                q2_buf[c * both + h * TILE:c * both + (h + 1) * TILE, :] = jnp.concatenate([high, low], axis=1)
            q2 = q2_buf[r, :]
            state = None
            for t in range(c, -1, -1):
                s = scores_of(q2, k_buf[t * TILE:(t + 1) * TILE, :])
                if t == c:
                    s = jnp.where(lower, s, NEG)
                state = fold(state, s, v_buf[t * TILE:(t + 1) * TILE, :], jnp.ones((TILE, HEAD_DIM), BF16))
            top[r, :], acc[r, :] = state

    def folded(t):
        r = pl.ds(pl.multiple_of(t * TILE, TILE), TILE)
        s = scores_of(q2_buf[...], kv[r, :HEAD_DIM])
        return fold((top[...], acc[...]), s, kv[r, HEAD_DIM:], ones[r, :])

    def compute(t):
        top[...], acc[...] = folded(t)

    def finish(total):
        for c in range(blk // TILE):
            for h in range(heads):
                r = slice(c * both + h * TILE, c * both + (h + 1) * TILE)
                o_ref[c * TILE:(c + 1) * TILE, h * HEAD_DIM:(h + 1) * HEAD_DIM] = (
                    total[r, :HEAD_DIM] / total[r, HEAD_DIM:]).astype(BF16)

    swap = remote(mine, other, s_sem.at[0], s_sem.at[1], at(z, (y + 2) % RING))

    def down_far(i):
        far = slot(RING + z + 1 + i + (RING - 1) * i + 1)
        return remote(other, far, f_send.at[i], y_recv.at[2, i], at(z + 1 + i, y))

    def far_from_above(i):
        return remote(other, cross_slot(i, 2), f_send.at[i], y_recv.at[2, i], at(z - 1 - i, y))

    def hand(a):
        return remote(anchor.at[pl.ds(a * quarter, quarter)], slot(RING + a), hand_send.at[a], a_recv.at[0], at(0, a))

    def to_row(c):
        return remote(mine, slot(y), r_send.at[c], r_recv.at[y], at(z, c))

    def from_row(c):
        return remote(mine, slot(c), r_send.at[c], r_recv.at[c], at(z, c))

    def down(t):
        return remote(mine, column_slot(t - 1 - z), z_send.at[t], z_recv.at[t - 1 - z], at(t, y))

    def from_above(i):
        return remote(mine, column_slot(i), z_send.at[0], z_recv.at[i], at(z - 1 - i, y))

    def down_anchor(t):
        return remote(slot(RING + y), slot(RING * (t + 1) + y), a_send.at[t], a_recv.at[0], at(t, y))

    def my_anchor():
        quarter_slot = slot(RING * (z + 1) + y)
        return remote(quarter_slot, quarter_slot, a_send.at[0], a_recv.at[0], at(z, (y + 1) % RING))

    def across(i, d):
        return remote(column_slot(i), cross_slot(i, d), y_send.at[d, i], y_recv.at[d, i], at(z, (y + d) % RING))

    def from_across(i, d):
        return remote(column_slot(i), cross_slot(i, d), y_send.at[d, i], y_recv.at[d, i], at(z, (y + RING - d) % RING))

    def across_anchor(d):
        quarter_slot = slot(RING * (z + 1) + y)
        return remote(quarter_slot, quarter_slot, ay_send.at[d], ay_recv.at[d], at(z, (y + d) % RING))

    def from_across_anchor(d):
        there = (y + RING - d) % RING
        quarter_slot = slot(RING * (z + 1) + there)
        return remote(quarter_slot, quarter_slot, ay_send.at[d], ay_recv.at[d], at(z, there))

    early = z < rows // 2

    @pl.when(z == 0)
    def _():
        pl.semaphore_wait(barrier, RING - 1)

        @pl.when(y == 0)
        def _():
            for a in range(1, RING):
                hand(a).start()

    @pl.when(early)
    def _():
        own_block()

    @pl.when(z == 0)
    def _():
        @pl.when(y > 0)
        def _():
            my_anchor().wait_recv()

        pl.semaphore_wait(ready, last)

    @pl.when(z > 0)
    def _():
        pl.semaphore_wait(barrier, last - z + RING)
        pl.semaphore_signal(ready, inc=1, device_id=at(0, y), device_id_type=MESH)

    swap.start()
    loop(0, last - z, lambda i: down(last - i).start())

    @pl.when(z == 0)
    def _():
        down_anchor(last).start()
        loop(1, last, lambda t: down_anchor(t).start())

    loop(y + 1, RING, lambda c: to_row(c).start())

    @pl.when(jnp.logical_not(early))
    def _():
        own_block()

    swap.wait_recv()
    doubled = 1 + (NEAR - 1) * (z // last)

    def each_far(go):
        @pl.when(z < last)
        def _():
            go(down_far(0))

        for i in range(1, NEAR):
            @pl.when(z + 1 + i == last)
            def _():
                go(down_far(i))

    each_far(lambda copy: copy.start())

    def forward(i):
        from_above(i).wait_recv()

        @pl.when(i >= doubled)
        def _():
            across(i, 2).start()

        for d in (1, 3):
            across(i, d).start()

    def forward_anchor():
        @pl.when(z > 0)
        def _():
            my_anchor().wait_recv()

        for d in (2, 1, 3):
            across_anchor(d).start()

    def need(t):
        @pl.when(t == 0)
        def _():
            loop(0, y, lambda c: from_row(c).wait_recv())

        @pl.when((t > 0) & (t <= z))
        def _():
            def one(k):
                u = RING * (t - 1) + k - z

                @pl.when(u >= 0)
                def _():
                    from_across(u // (RING - 1), 1 + u % (RING - 1)).wait_recv()

            loop(0, RING, one)

        @pl.when(t == z + 1)
        def _():
            for d in range(1, RING):
                from_across_anchor(d).wait_recv()

    low = z // (rows // 2)

    def step(k):
        late = (k + rows - z) // rows
        tile = k + low * late * (1 - 2 * (k - z))

        @pl.when(k > 0)
        def _():
            loop(jnp.minimum(z, AHEAD * (k - 1)), jnp.minimum(z, AHEAD * k), forward)

        @pl.when(k == 1 + 2 * low)
        def _():
            forward_anchor()

        need(tile)
        return tile

    def work(k):
        tile = step(k)

        @pl.when((me > 0) & (k + y > 0))
        def _():
            compute(tile)

    loop(0, z + 1, work)
    final = step(z + 1)

    @pl.when(me > 0)
    def _():
        finish(folded(final)[1])

    @pl.when(me == 0)
    def _():
        finish(acc[...])

    def gone(i):
        @pl.when(i >= doubled)
        def _():
            across(i, 2).wait_send()

        for d in (1, 3):
            across(i, d).wait_send()

    loop(0, z, gone)
    swap.wait_send()
    each_far(lambda copy: copy.wait_send())
    for d in range(1, RING):
        across_anchor(d).wait_send()
    loop(y + 1, RING, lambda c: to_row(c).wait_send())
    loop(z + 1, rows, lambda t: down(t).wait_send())

    @pl.when(z == 0)
    def _():
        loop(1, rows, lambda t: down_anchor(t).wait_send())

    @pl.when(me == 0)
    def _():
        for a in range(1, RING):
            hand(a).wait_send()


def on_device(hosts, queries, keys, values, kept):
    blk, width = queries.shape
    heads = width // HEAD_DIM
    ret = kept.shape[2]
    rows = hosts // RING
    hbm = pl.BlockSpec(memory_space=pltpu.HBM)
    dma = pltpu.SemaphoreType.DMA
    return pl.pallas_call(
        functools.partial(kernel, rows, heads),
        out_shape=pltpu.VMEM((blk, width), BF16),
        in_specs=[hbm] * 4,
        out_specs=pl.BlockSpec(memory_space=pltpu.VMEM),
        scratch_shapes=[
            pltpu.VMEM((blk, width), BF16),
            pltpu.VMEM((blk, HEAD_DIM), BF16),
            pltpu.VMEM((blk, HEAD_DIM), BF16),
            pltpu.VMEM((1, ret), jnp.int32),
            pltpu.VMEM((blk * heads, 2 * HEAD_DIM), BF16),
            pltpu.VMEM(((rows + 1) * TILE, 2 * HEAD_DIM), BF16),
            pltpu.VMEM((ANCHOR_TOKENS, 2 * HEAD_DIM), BF16),
            pltpu.VMEM(((rows + 1) * TILE, HEAD_DIM), BF16),
            pltpu.VMEM((ret, 2 * HEAD_DIM), BF16),
            pltpu.VMEM((ret, 2 * HEAD_DIM), BF16),
            pltpu.VMEM((blk * heads, 2 * HEAD_DIM), F32),
            pltpu.VMEM((blk * heads, HEAD_DIM), F32),
            dma((4,)),
            pltpu.SemaphoreType.REGULAR,
            dma((rows,)), dma((rows,)), dma((RING, rows)), dma((RING, rows)),
            dma((RING,)), dma((RING,)), dma((2,)), dma((NEAR,)), dma((RING,)),
            dma((1,)), dma((rows,)), dma((RING,)), dma((RING,)),
        ],
        compiler_params=pltpu.CompilerParams(
            collective_id=0, has_side_effects=True, vmem_limit_bytes=61 * 2**20),
    )(queries, keys, values, kept[0])


def solution(mesh):
    placed = (P("ctx", "head"), P("ctx", "head"), P("ctx", "head"), P("head", "ctx", None))
    return jax.shard_map(
        functools.partial(on_device, mesh.shape["ctx"]), mesh=mesh, in_specs=placed,
        out_specs=P("ctx", "head"), check_vma=False)
```
